32 devices in a mesh: sec: 4 (over y, core), gy: 2 (over x), gx: 4 (over z).
Axes of the slice: x: 2, y: 2, z: 4, core: 2. Of those that a mesh axis runs over, the one named last changes fastest.
Arguments:
- sections: bfloat16 [4, 320, 640], P('sec', 'gy', 'gx'), may hold values from -16 to 16
- first_kernel: bfloat16 [32, 9], replicated, may hold values from -2 to 2
- first_bias: bfloat16 [32], replicated, may hold values from -3 to 3
- second_kernel: bfloat16 [32, 288], replicated, may hold values from -0.375 to 0.375
- second_bias: bfloat16 [32], replicated, may hold values from -3 to 3
- coarse: int32 [4, 2], P('sec'), may hold values from -4 to 4
- tissue: int32 [4, 2, 4], P('sec', 'gy', 'gx'), may hold values 0 or 1
Outputs:
- features: bfloat16 [4, 320, 20480], P('sec', 'gy', 'gx')
- flow: float32 [4, 3, 2, 2, 4], P('sec', None, None, 'gy', 'gx')
- displacement: float32 [4, 2, 2, 4], P('sec', None, 'gy', 'gx')
The draws below stay inside these ranges and needn't reach their ends.
All inputs are finite; a program needn't handle non-finite values. No bound on the sum of `tissue` on one device may be relied on, other than what follows from the above.
Results may differ from the reference program's by a relative error of at most 0.0043.
Values may be sent and summed in bfloat16 or wider, within the bound.
A program may use at most 128 MiB of HBM per device.

```python
import jax
import jax.numpy as jnp
from jax import lax

PATCH = 160
CHANNELS = 32
LAGS = 3
STEPS = 2
SECS = 4
TILE_ROWS = 2
TILE_COLS = 4
PIX_ROWS = 320
PIX_COLS = 640


def draw_sections(key, part):
    key = jax.random.fold_in(key, 11)
    texture_key, drift_key, speckle_key = jax.random.split(key, 3)
    reach = PATCH // 8
    drift_steps = jax.random.randint(drift_key, (SECS, 2, TILE_ROWS, TILE_COLS), -reach, reach + 1)
    offsets = jnp.cumsum(drift_steps, axis=0)
    rows_ramp = jnp.arange(PIX_ROWS, dtype=jnp.int32)
    cols_ramp = jnp.arange(PIX_COLS, dtype=jnp.int32)
    row_tile = rows_ramp // PATCH
    col_tile = cols_ramp // PATCH
    shift_rows = offsets[:, 0][:, row_tile][:, :, col_tile]
    shift_cols = offsets[:, 1][:, row_tile][:, :, col_tile]
    source_rows = (rows_ramp[None, :, None] - shift_rows) % PIX_ROWS
    source_cols = (cols_ramp[None, None, :] - shift_cols) % PIX_COLS
    speckle = jax.random.normal(speckle_key, (SECS, PIX_ROWS, PIX_COLS), jnp.float32)
    texture = jax.random.normal(texture_key, (PIX_ROWS, PIX_COLS), jnp.float32)
    contrast = 0.35
    picked = texture[source_rows, source_cols]
    image = contrast * picked + speckle
    return jnp.clip(image, -16.0, 16.0).astype(jnp.bfloat16)


def touch_ends(values, key, smallest, top_value):
    dims = values.shape
    spot = [jax.random.randint(jax.random.fold_in(key, axis), (), 0, dims[axis]) for axis in range(len(dims))]
    values = values.at[tuple(spot)].set(smallest)
    longest = dims.index(max(dims))
    spot[longest] = (spot[longest] + 1) % dims[longest]
    return values.at[tuple(spot)].set(top_value)


def normal_values(key, dims, scale, limit, held_as=jnp.bfloat16):
    return jnp.clip(scale * jax.random.normal(key, dims, jnp.float32), -limit, limit).astype(held_as)


def setup_inputs(seed: int = 0) -> dict:
    streams_of = jax.random.split(jax.random.key(seed), 8)
    return {
        "sections": draw_sections(jax.random.fold_in(streams_of[7], 71), 0),
        "first_kernel": normal_values(streams_of[1], (CHANNELS, 9), 9 ** -0.5, 2.0),
        "first_bias": normal_values(streams_of[2], (CHANNELS,), 0.5, 3.0),
        "second_kernel": normal_values(streams_of[3], (CHANNELS, 9 * CHANNELS), (9 * CHANNELS) ** -0.5, 0.375),
        "second_bias": normal_values(streams_of[4], (CHANNELS,), 0.5, 3.0),
        "coarse": touch_ends(jax.random.randint(streams_of[5], (SECS, 2), -4, 5), jax.random.fold_in(streams_of[5], 1), -4, 4).astype(jnp.int32),
        "tissue": touch_ends((jax.random.randint(streams_of[6], (SECS, TILE_ROWS, TILE_COLS), 0, 8) < 7).astype(jnp.int32), jax.random.fold_in(streams_of[6], 1), 0, 1),
    }


LAG_WEIGHTS = (1.0, 0.5, 0.25)
STEP_SIZE = 0.3
PLANE_STIFF = 0.5
HIGHEST_MODE = lax.Precision.HIGHEST


def rounded(values):
    return lax.optimization_barrier(values.astype(jnp.bfloat16)).astype(jnp.float32)


def tables(length):
    ramp = jnp.arange(length, dtype=jnp.int32)
    phase = (ramp[:, None] * ramp[None, :]) % length
    angle = phase.astype(jnp.float32) * (2.0 * 3.141592653589793 / length)
    return jnp.cos(angle), jnp.sin(angle)


def encode_all(sections, first_kernel, first_bias, second_kernel, second_bias):
    numbers = ('NCHW', 'OIHW', 'NCHW')
    first = first_kernel.astype(jnp.float32).reshape(CHANNELS, 1, 3, 3)
    second = second_kernel.astype(jnp.float32).reshape(CHANNELS, 3, 3, CHANNELS).transpose(0, 3, 1, 2)

    def one_section(section_image):
        summed = lax.conv_general_dilated(section_image.astype(jnp.float32)[None, None], first, (1, 1), 'SAME', dimension_numbers=numbers, precision=HIGHEST_MODE)[0]
        hidden = rounded(jax.nn.silu(summed + first_bias.astype(jnp.float32)[:, None, None]))
        result = lax.conv_general_dilated(hidden[None], second, (1, 1), 'SAME', dimension_numbers=numbers, precision=HIGHEST_MODE)[0]
        return (result + second_bias.astype(jnp.float32)[:, None, None]).astype(jnp.bfloat16)

    return lax.map(one_section, sections)


def spectrum(features, first_table, left_table):
    rowwise = rounded(jnp.einsum('chv,vpw->chpw', features.astype(jnp.float32), first_table, precision=HIGHEST_MODE))
    both = jnp.einsum('qjph,chpw->cqjw', left_table, rowwise, precision=HIGHEST_MODE)
    return lax.optimization_barrier(both.astype(jnp.bfloat16))


def product(left, right):
    return jnp.dot(left, right, precision=HIGHEST_MODE)


def soft_peak(current, earlier, cosine_table, sine_table, signed):
    channels = current.shape[0]
    length = current.shape[-1]
    cur_re = current[:, 0].astype(jnp.float32)
    cur_im = current[:, 1].astype(jnp.float32)
    ear_re = earlier[:, 0].astype(jnp.float32)
    ear_im = earlier[:, 1].astype(jnp.float32)
    power_re = jnp.sum(ear_re * cur_re + ear_im * cur_im, axis=0)
    power_im = jnp.sum(ear_re * cur_im - ear_im * cur_re, axis=0)
    mixed_re = product(cosine_table, power_re) - product(sine_table, power_im)
    mixed_im = product(sine_table, power_re) + product(cosine_table, power_im)
    surface = (product(mixed_re, cosine_table) - product(mixed_im, sine_table)) / (length * length)
    scores = surface / (channels * length)
    chances = jax.nn.softmax(scores.reshape(-1)).reshape(length, length)
    flow_y = jnp.sum(chances * signed[:, None])
    flow_x = jnp.sum(chances * signed[None, :])
    return jnp.stack([flow_y, flow_x])


def reference(sections, first_kernel, first_bias, second_kernel, second_bias, coarse, tissue):
    features = encode_all(sections, first_kernel, first_bias, second_kernel, second_bias)
    cosine_table, sine_table = tables(PATCH)
    first_table = rounded(jnp.stack([cosine_table, sine_table], axis=1))
    left_table = rounded(jnp.stack([jnp.stack([cosine_table, -sine_table], axis=1), jnp.stack([-sine_table, -cosine_table], axis=1)], axis=0))
    signed = ((jnp.arange(PATCH, dtype=jnp.int32) + PATCH // 2) % PATCH - PATCH // 2).astype(jnp.float32)
    zero_start = jnp.zeros((), jnp.int32)

    def one_tile(position):
        tile_row = position // TILE_COLS
        tile_col = position % TILE_COLS
        block = lax.dynamic_slice(features, (zero_start, zero_start, tile_row * PATCH, tile_col * PATCH), (SECS, CHANNELS, PATCH, PATCH))
        spectra = [spectrum(block[section], first_table, left_table) for section in range(SECS)]
        per_section = []
        for section in range(SECS):
            per_lag = []
            for lag_step in range(1, LAGS + 1):
                if section >= lag_step:
                    per_lag.append(soft_peak(spectra[section], spectra[section - lag_step], cosine_table, sine_table, signed))
                else:
                    per_lag.append(jnp.zeros((2,), jnp.float32))
            per_section.append(jnp.stack(per_lag))
        return jnp.stack(per_section)

    flows = lax.map(one_tile, jnp.arange(TILE_ROWS * TILE_COLS, dtype=jnp.int32))
    flows = flows.reshape(TILE_ROWS, TILE_COLS, SECS, LAGS, 2).transpose(2, 3, 4, 0, 1)

    coarse_float = coarse.astype(jnp.float32)
    tissue_float = tissue.astype(jnp.float32)
    weight_list = []
    target_list = []
    for lag_step in range(1, LAGS + 1):
        prior_tissue = jnp.concatenate([jnp.zeros((lag_step, TILE_ROWS, TILE_COLS), jnp.float32), tissue_float[:-lag_step]], axis=0)
        prior_coarse = jnp.concatenate([jnp.zeros((lag_step, 2), jnp.float32), coarse_float[:-lag_step]], axis=0)
        weight_list.append(LAG_WEIGHTS[lag_step - 1] * tissue_float * prior_tissue)
        target_list.append(flows[:, lag_step - 1] + (coarse_float - prior_coarse)[:, :, None, None])
    rows_ramp = jnp.arange(TILE_ROWS, dtype=jnp.int32)
    cols_ramp = jnp.arange(TILE_COLS, dtype=jnp.int32)
    count = ((rows_ramp > 0).astype(jnp.float32) + (rows_ramp < TILE_ROWS - 1).astype(jnp.float32))[:, None] + ((cols_ramp > 0).astype(jnp.float32) + (cols_ramp < TILE_COLS - 1).astype(jnp.float32))[None, :]
    nodes = jnp.broadcast_to(coarse_float[:, :, None, None], (SECS, 2, TILE_ROWS, TILE_COLS))
    for relax_step in range(STEPS):
        pulled = jnp.zeros((SECS, 2, TILE_ROWS, TILE_COLS), jnp.float32)
        for lag_step in range(1, LAGS + 1):
            before = jnp.concatenate([jnp.zeros((lag_step, 2, TILE_ROWS, TILE_COLS), jnp.float32), nodes[:-lag_step]], axis=0)
            pulled = pulled + weight_list[lag_step - 1][:, None] * (before + target_list[lag_step - 1] - nodes)
        padded = jnp.pad(nodes, ((0, 0), (0, 0), (1, 1), (1, 1)))
        beside_all = padded[:, :, :-2, 1:-1] + padded[:, :, 2:, 1:-1] + padded[:, :, 1:-1, :-2] + padded[:, :, 1:-1, 2:]
        nodes = nodes + STEP_SIZE * (pulled + PLANE_STIFF * (beside_all - count * nodes))
    features_out = features.transpose(0, 2, 3, 1).reshape(SECS, PIX_ROWS, PIX_COLS * CHANNELS)
    return (features_out, flows, nodes)
```

```python
import jax
import jax.numpy as jnp
import numpy as np
from jax import lax
from jax.experimental import pallas as pl
from jax.experimental.pallas import tpu as pltpu
from jax.sharding import PartitionSpec as P

LAGS = 3

LAG_WEIGHTS = (1.0, 0.5, 0.25)
STEP_SIZE = 0.3
PLANE_STIFF = 0.5
SPAN = 16
HALF = 128
BF = jnp.bfloat16
F32 = jnp.float32


def extended(cells, sides, width):
    for axis, dim in sides:
        count = lax.axis_size(axis)
        ends = count - 1
        head = lax.slice_in_dim(cells, 0, width, axis=dim)
        tail = lax.slice_in_dim(cells, cells.shape[dim] - width, cells.shape[dim], axis=dim)
        cells = jnp.concatenate(
            [
                lax.ppermute(tail, axis, [(i, (i + 1) % count) for i in range(ends)]),
                cells,
                lax.ppermute(head, axis, [((i + 1) % count, i) for i in range(ends)]),
            ],
            axis=dim,
        )
    return cells


def shifted(value, axis, by):
    count = lax.axis_size(axis)
    pairs = [(i, i + by) for i in range(count) if 0 <= i + by < count]
    return lax.ppermute(value, axis, pairs)


def make_tables(length, parts):
    ramp = np.arange(length)
    angle = (ramp[:, None] * ramp[None, :] % length) * (2.0 * np.pi / length)
    cos, sin = np.cos(angle), np.sin(angle)
    kept = length // 2 + 1
    first = np.zeros((length, 2 * HALF))
    first[:, :kept] = cos[:, :kept]
    first[:, HALF : HALF + kept] = sin[:, :kept]
    chunk = length // parts
    left, back = [], []
    for q in range(parts):
        rows = slice(q * chunk, (q + 1) * chunk)
        left += [np.concatenate([cos[rows], -sin[rows]], 1), np.concatenate([-sin[rows], -cos[rows]], 1)]
        back += [np.concatenate([cos[:, rows], sin[:, rows]], 0), np.concatenate([-sin[:, rows], cos[:, rows]], 0)]
    times = np.full((kept, 1), 2.0)
    times[0] = times[-1] = 1.0
    last = np.zeros((2 * HALF, length))
    last[:kept] = times * cos[:kept]
    last[HALF : HALF + kept] = -times * sin[:kept]
    return (
        first.astype(np.float32),
        np.concatenate(left, 0).astype(np.float32),
        np.concatenate(back, 1).astype(np.float32),
        last.astype(np.float32),
    )


def silu(values):
    half = 0.5 * values
    return half + half * jnp.tanh(half)


def encode_kernel(
    edge, across, down, band1, band1t, band2, band2t, bias1, bias1t, bias2, bias2t, first, left,
    feat, spec, hid, hidt, rowwise,
):
    length = feat.shape[0]
    wide = across.shape[-1]
    ylo, yhi, xlo, xhi = edge[0], edge[1], edge[2], edge[3]
    lanes = band1.shape[1]
    channels = lanes // SPAN
    shift = channels.bit_length() - 1

    def first_layer(blk, carry):
        r0 = pl.multiple_of(blk * SPAN, SPAN)
        c0 = pl.multiple_of(blk * lanes, lanes)
        rhs = jnp.concatenate([down[a, pl.ds(r0, 2 * SPAN), :] for a in range(3)], axis=0)
        summed = lax.dot_general(rhs, band1[...], (((0,), (0,)), ((), ())), preferred_element_type=F32)
        row = lax.broadcasted_iota(jnp.int32, (wide, 1), 0)
        col = r0 + lax.shift_right_logical(lax.broadcasted_iota(jnp.int32, (1, lanes), 1), shift)
        keep = ((row >= ylo) & (row <= yhi)).astype(F32) * ((col >= xlo) & (col <= xhi)).astype(F32)
        value = silu(summed + bias1[...]) * keep
        for a in range(3):
            hid[a, :, pl.ds(c0, lanes)] = value[a : a + length].astype(BF)

        rhs = jnp.concatenate([across[b, pl.ds(r0, 2 * SPAN), :] for b in range(3)], axis=0)
        summed = jnp.dot(band1t[...], rhs, preferred_element_type=F32)
        row = r0 + lax.shift_right_logical(lax.broadcasted_iota(jnp.int32, (lanes, 1), 0), shift)
        col = lax.broadcasted_iota(jnp.int32, (1, wide), 1)
        keep = ((row >= ylo) & (row <= yhi)).astype(F32) * ((col >= xlo) & (col <= xhi)).astype(F32)
        value = silu(summed + bias1t[...]) * keep
        for b in range(3):
            hidt[b, pl.ds(c0, lanes), :] = value[:, b : b + length].astype(BF)
        return carry

    lax.fori_loop(0, wide // SPAN, first_layer, 0)
    cols = band2.shape[2]
    depth = band2.shape[1]

    def second_layer(blk, carry):
        c0 = pl.multiple_of(blk * cols, cols)
        acc = bias2[...] + jnp.dot(hid[0, :, pl.ds(c0, depth)], band2[0], preferred_element_type=F32)
        for a in range(1, 3):
            acc = acc + jnp.dot(hid[a, :, pl.ds(c0, depth)], band2[a], preferred_element_type=F32)
        feat[:, pl.ds(c0, cols)] = acc.astype(BF)
        acc = bias2t[...] + jnp.dot(band2t[0], hidt[0, pl.ds(c0, depth), :], preferred_element_type=F32)
        for b in range(1, 3):
            acc = acc + jnp.dot(band2t[b], hidt[b, pl.ds(c0, depth), :], preferred_element_type=F32)
        pair = jnp.dot(acc.astype(BF), first[...], preferred_element_type=F32)
        rowwise[0, pl.ds(c0, cols), :] = pair[:, :HALF]
        rowwise[1, pl.ds(c0, cols), :] = pair[:, HALF:]
        return carry

    lax.fori_loop(0, length * channels // cols, second_layer, 0)
    parts = spec.shape[0]
    size = spec.shape[2]

    def columns(step, carry):
        c = step * 2
        both = jnp.concatenate(
            [
                jnp.concatenate(
                    [rowwise[q, pl.ds(c + i, length, stride=channels), :].astype(BF) for q in range(2)],
                    axis=0,
                )
                for i in range(2)
            ],
            axis=1,
        )
        out = jnp.dot(left[...], both, preferred_element_type=F32).astype(BF)
        for q in range(parts):
            for i in range(2):
                spec[q, c + i] = out[q * size : (q + 1) * size, i * HALF : (i + 1) * HALF]
        return carry

    lax.fori_loop(0, channels // 2, columns, 0)


def power_kernel(got, out):
    secs, channels, size, lanes = got.shape
    half = size // 2
    out[...] = jnp.zeros_like(out)

    def channel(c, carry):
        values = [got[t, c].astype(F32) for t in range(secs)]
        for s in range(secs):
            for lag in range(1, min(s, LAGS) + 1):
                cur, ear = values[s], values[s - lag]
                out[s, lag - 1, :half] += ear[:half] * cur[:half] + ear[half:] * cur[half:]
                out[s, lag - 1, half:] += ear[:half] * cur[half:] - ear[half:] * cur[:half]
        return carry

    lax.fori_loop(0, channels, channel, 0)


def peak_kernel(scale, power, back, last, flow):
    parts = power.shape[0]
    length = last.shape[1]
    row = lax.broadcasted_iota(jnp.int32, (length, 1), 0)
    col = lax.broadcasted_iota(jnp.int32, (1, length), 1)
    sign_y = jnp.where(row < length // 2, row, row - length).astype(F32)
    sign_x = jnp.where(col < length // 2, col, col - length).astype(F32)
    place = lax.broadcasted_iota(jnp.int32, flow.shape, 0)
    side = lax.broadcasted_iota(jnp.int32, flow.shape, 1)
    result = jnp.zeros(flow.shape, F32)
    stacked = jnp.concatenate(
        [jnp.concatenate([power[q, lag] for q in range(parts)], axis=0) for lag in range(LAGS)], axis=1
    )
    mixed = jnp.dot(back[...], stacked, precision=lax.Precision.HIGHEST, preferred_element_type=F32)
    for lag in range(LAGS):
        part = mixed[:, lag * HALF : (lag + 1) * HALF]
        lhs = jnp.concatenate([part[:length], part[length:]], axis=1)
        scores = jnp.dot(lhs, last[...], precision=lax.Precision.HIGHEST, preferred_element_type=F32) * scale
        chances = jnp.exp(scores - jnp.max(scores))
        total = jnp.sum(chances)
        flow_y = jnp.sum(chances * sign_y) / total
        flow_x = jnp.sum(chances * sign_x) / total
        result = jnp.where((place == lag) & (side == 0), flow_y, result)
        result = jnp.where((place == lag) & (side == 1), flow_x, result)
    flow[...] = result


def bands(first_kernel, second_kernel):
    channels = first_kernel.shape[0]
    delta = np.arange(2 * SPAN)[:, None] - np.arange(SPAN)[None, :]
    hot1 = jnp.asarray(np.stack([delta == t for t in range(3)]).astype(np.float32), BF)
    taps = first_kernel.reshape(channels, 3, 3)
    band1 = jnp.einsum("txl,kat->axlk", hot1, taps).reshape(6 * SPAN, SPAN * channels)
    band1t = jnp.einsum("tyl,ktb->lkby", hot1, taps).reshape(SPAN * channels, 6 * SPAN)
    short = SPAN // 2
    delta = np.arange(12)[:, None] - np.arange(short)[None, :]
    hot2 = jnp.asarray(np.stack([delta == t for t in range(3)]).astype(np.float32), BF)
    taps = second_kernel.reshape(channels, 3, 3, channels)
    band2 = jnp.einsum("txl,catk->axklc", hot2, taps).reshape(3, 12 * channels, short * channels)
    band2t = jnp.einsum("tyl,ctbk->blcyk", hot2, taps).reshape(3, short * channels, 12 * channels)
    return band1, band1t, band2, band2t


def body(sections, first_kernel, first_bias, second_kernel, second_bias, coarse, tissue):
    length = sections.shape[-1]
    channels = first_kernel.shape[0]
    secs = lax.axis_size("sec")
    first, left, back, last = make_tables(length, secs)
    row_index = lax.axis_index("gy")
    col_index = lax.axis_index("gx")
    rows_count = lax.axis_size("gy")
    cols_count = lax.axis_size("gx")
    sec_index = lax.axis_index("sec")

    band1, band1t, band2, band2t = bands(first_kernel, second_kernel)
    bias1 = jnp.tile(first_bias.astype(F32), SPAN)
    bias2 = jnp.tile(second_bias.astype(F32), SPAN // 2)
    metadata = jnp.concatenate([tissue.reshape(1), coarse.reshape(2)]).astype(BF)
    prior_all = [shifted(metadata, "sec", lag).astype(F32) for lag in range(1, LAGS + 1)]

    wide = length + SPAN
    image = extended(sections, (("gy", 1), ("gx", 2)), 2)[0]
    pad = wide + SPAN + 2 - image.shape[0]
    image = jnp.pad(image, ((0, pad), (0, pad)))
    across = jnp.stack([image[: wide + SPAN, b : b + wide] for b in range(3)])
    turned = image.T
    down = jnp.stack([turned[: wide + SPAN, a : a + wide] for a in range(3)])
    edge = jnp.stack(
        [
            jnp.where(row_index == 0, 1, 0),
            jnp.where(row_index == rows_count - 1, length, length + 1),
            jnp.where(col_index == 0, 1, 0),
            jnp.where(col_index == cols_count - 1, length, length + 1),
        ]
    ).astype(jnp.int32)
    vmem = pl.BlockSpec(memory_space=pltpu.VMEM)
    size = 2 * length // secs
    features, spec = pl.pallas_call(
        encode_kernel,
        out_shape=(
            jax.ShapeDtypeStruct((length, length * channels), BF),
            jax.ShapeDtypeStruct((secs, channels, size, HALF), BF),
        ),
        in_specs=[pl.BlockSpec(memory_space=pltpu.SMEM)] + [vmem] * 12,
        out_specs=(vmem, vmem),
        scratch_shapes=[
            pltpu.VMEM((3, length, wide * channels), BF),
            pltpu.VMEM((3, wide * channels, length), BF),
            pltpu.VMEM((2, length * channels, HALF), F32),
        ],
        compiler_params=pltpu.CompilerParams(vmem_limit_bytes=48 * 1024 * 1024),
        name="encode",
    )(
        edge, across, down, band1, band1t, band2, band2t,
        bias1[None, :], bias1[:, None], bias2[None, :], bias2[:, None],
        jnp.asarray(first, BF), jnp.asarray(left, BF),
    )

    got = lax.all_to_all(spec, "sec", 0, 0)
    power = pl.pallas_call(
        power_kernel,
        out_shape=jax.ShapeDtypeStruct((secs, LAGS, size, HALF), F32),
        in_specs=[vmem],
        out_specs=vmem,
        compiler_params=pltpu.CompilerParams(vmem_limit_bytes=32 * 1024 * 1024),
        name="power",
    )(got)
    power = lax.all_to_all(power, "sec", 0, 0)
    scale = 1.0 / (float(length) ** 3 * channels)
    peaks = pl.pallas_call(
        lambda *refs: peak_kernel(scale, *refs),
        out_shape=jax.ShapeDtypeStruct((8, 128), F32),
        in_specs=[vmem] * 3,
        out_specs=vmem,
        compiler_params=pltpu.CompilerParams(vmem_limit_bytes=32 * 1024 * 1024),
        name="peak",
    )(power, jnp.asarray(back), jnp.asarray(last))
    reach = jnp.arange(1, LAGS + 1, dtype=jnp.int32)
    flows = jnp.where((sec_index >= reach)[:, None], peaks[:LAGS, :2], 0.0)

    own_mask = tissue.reshape(()).astype(F32)
    own = coarse.reshape(2).astype(F32)
    weights = [
        jnp.where(sec_index >= lag, LAG_WEIGHTS[lag - 1] * own_mask * prior_all[lag - 1][0], 0.0)
        for lag in range(1, LAGS + 1)
    ]
    targets = [flows[lag - 1] + own - prior_all[lag - 1][1:] for lag in range(1, LAGS + 1)]
    pulled = jnp.zeros_like(own)
    for lag in range(1, LAGS + 1):
        pulled = pulled + weights[lag - 1] * (prior_all[lag - 1][1:] + targets[lag - 1] - own)
    nodes = own + STEP_SIZE * pulled
    count = (
        (row_index > 0).astype(F32)
        + (row_index < rows_count - 1).astype(F32)
        + (col_index > 0).astype(F32)
        + (col_index < cols_count - 1).astype(F32)
    )
    pulled = jnp.zeros_like(own)
    for lag in range(1, LAGS + 1):
        pulled = pulled + weights[lag - 1] * (shifted(nodes, "sec", lag) + targets[lag - 1] - nodes)
    beside = shifted(nodes, "gy", 1) + shifted(nodes, "gy", -1) + shifted(nodes, "gx", 1) + shifted(nodes, "gx", -1)
    nodes = nodes + STEP_SIZE * (pulled + PLANE_STIFF * (beside - count * nodes))
    return (
        features.reshape(1, length, features.shape[-1]),
        flows.reshape(1, LAGS, 2, 1, 1),
        nodes.reshape(1, 2, 1, 1),
    )


def solution(mesh):
    in_specs = (P("sec", "gy", "gx"), P(), P(), P(), P(), P("sec", None), P("sec", "gy", "gx"))
    out_specs = (P("sec", "gy", "gx"), P("sec", None, None, "gy", "gx"), P("sec", None, "gy", "gx"))
    return jax.shard_map(body, mesh=mesh, in_specs=in_specs, out_specs=out_specs, check_vma=False)
```

```python
import functools

import jax
import jax.numpy as jnp
import numpy as np
from jax import lax
from jax.experimental import pallas as pl
from jax.experimental.pallas import tpu as pltpu
from jax.sharding import PartitionSpec as P

LAGS = 3

LAG_WEIGHTS = (1.0, 0.5, 0.25)
STEP_SIZE = 0.3
PLANE_STIFF = 0.5
SPAN = 16
HALF = 128
BF = jnp.bfloat16
F32 = jnp.float32


def extended(cells, sides, width):
    for axis, dim in sides:
        count = lax.axis_size(axis)
        ends = count - 1
        head = lax.slice_in_dim(cells, 0, width, axis=dim)
        tail = lax.slice_in_dim(cells, cells.shape[dim] - width, cells.shape[dim], axis=dim)
        cells = jnp.concatenate(
            [
                lax.ppermute(tail, axis, [(i, (i + 1) % count) for i in range(ends)]),
                cells,
                lax.ppermute(head, axis, [((i + 1) % count, i) for i in range(ends)]),
            ],
            axis=dim,
        )
    return cells


def make_tables(length, parts):
    ramp = np.arange(length)
    angle = (ramp[:, None] * ramp[None, :] % length) * (2.0 * np.pi / length)
    cos, sin = np.cos(angle), np.sin(angle)
    kept = length // 2 + 1
    first = np.zeros((length, 2 * HALF))
    first[:, :kept] = cos[:, :kept]
    first[:, HALF : HALF + kept] = sin[:, :kept]
    chunk = length // parts
    left, back = [], []
    for q in range(parts):
        rows = slice(q * chunk, (q + 1) * chunk)
        left += [np.concatenate([cos[rows], -sin[rows]], 1), np.concatenate([-sin[rows], -cos[rows]], 1)]
        back += [np.concatenate([cos[:, rows], sin[:, rows]], 0), np.concatenate([-sin[:, rows], cos[:, rows]], 0)]
    times = np.full((kept, 1), 2.0)
    times[0] = times[-1] = 1.0
    last = np.zeros((2 * HALF, length))
    last[:kept] = times * cos[:kept]
    last[HALF : HALF + kept] = -times * sin[:kept]
    return (
        first.astype(np.float32),
        np.concatenate(left, 0).astype(np.float32),
        np.concatenate(back, 1).astype(np.float32),
        last.astype(np.float32),
    )


def silu(values):
    half = 0.5 * values
    return half + half * jnp.tanh(half)


def tiled_eye(channels, lanes):
    lane = lax.broadcasted_iota(jnp.int32, (channels, lanes), 1)
    row = lax.broadcasted_iota(jnp.int32, (channels, lanes), 0)
    return ((lane & (channels - 1)) == row).astype(F32)


def across_rows(left, right):
    return lax.dot_general(left, right, (((0,), (0,)), ((), ())), preferred_element_type=F32)


def encode_kernel(
    across, down, kernel1, kernel2, bias1_in, bias2_in, first,
    feat, rowwise, hid, hidt, band1, band1t, band2, band2t, bias1, bias1t, bias2, bias2t,
):
    length = feat.shape[0]
    wide = across.shape[-1]
    lanes = band1.shape[1]
    cols = band2.shape[2]
    depth = band2.shape[1]
    channels = lanes // SPAN
    shift = channels.bit_length() - 1
    row_index, col_index = lax.axis_index("gy"), lax.axis_index("gx")
    ylo = jnp.where(row_index == 0, 1, 0)
    yhi = jnp.where(row_index == lax.axis_size("gy") - 1, length, length + 1)
    xlo = jnp.where(col_index == 0, 1, 0)
    xhi = jnp.where(col_index == lax.axis_size("gx") - 1, length, length + 1)

    eye = tiled_eye(channels, lanes)
    eye_bf = eye.astype(BF)
    for source, row_ref, col_ref, width in ((bias1_in, bias1, bias1t, lanes), (bias2_in, bias2, bias2t, cols)):
        spread = jnp.broadcast_to(source[...].astype(F32), (8, channels)).astype(BF)
        row = jnp.dot(spread, eye_bf[:, :width], preferred_element_type=F32)
        row_ref[...] = row
        col_ref[...] = jnp.transpose(jnp.broadcast_to(row[0:1], (128, width)))
    tap1 = across_rows(kernel1[...], eye_bf)
    unit = lax.shift_right_logical(lax.broadcasted_iota(jnp.int32, (2 * SPAN, lanes), 1), shift)
    gap = lax.broadcasted_iota(jnp.int32, (2 * SPAN, lanes), 0) - unit
    for ref, outer, inner in ((band1, 3, 1), (band1t, 1, 3)):
        parts = []
        for p in range(3):
            part = jnp.zeros((2 * SPAN, lanes), F32)
            for q in range(3):
                tap = outer * p + inner * q
                part = jnp.where(gap == q, tap1[tap : tap + 1], part)
            parts.append(part)
        whole = jnp.concatenate(parts, axis=0)
        if outer == 1:
            whole = jnp.transpose(whole)
        ref[...] = whole.astype(BF)
    tap2 = across_rows(kernel2[...], eye_bf[:, :cols])
    unit = lax.shift_right_logical(lax.broadcasted_iota(jnp.int32, (channels, cols), 1), shift)
    for a in range(3):
        for x in range(depth // channels):
            part = jnp.zeros((channels, cols), F32)
            for b in range(3):
                row = (3 * a + b) * channels
                part = jnp.where(unit == x - b, tap2[row : row + channels], part)
            band2[a, x * channels : (x + 1) * channels, :] = part.astype(BF)
    unit = lax.shift_right_logical(lax.broadcasted_iota(jnp.int32, (channels, depth), 1), shift)
    for b in range(3):
        taps = []
        for a in range(3):
            at = (3 * a + b) * channels
            taps.append(jnp.dot(kernel2[:, at : at + channels], eye_bf[:, :depth], preferred_element_type=F32))
        for y in range(cols // channels):
            part = jnp.zeros((channels, depth), F32)
            for a in range(3):
                part = jnp.where(unit == y + a, taps[a], part)
            band2t[b, y * channels : (y + 1) * channels, :] = part.astype(BF)

    def first_layer(blk, carry):
        r0 = pl.multiple_of(blk * SPAN, SPAN)
        c0 = pl.multiple_of(blk * lanes, lanes)
        rhs = jnp.concatenate([down[a, pl.ds(r0, 2 * SPAN), :] for a in range(3)], axis=0)
        summed = across_rows(rhs, band1[...])
        row = lax.broadcasted_iota(jnp.int32, (wide, 1), 0)
        col = r0 + lax.shift_right_logical(lax.broadcasted_iota(jnp.int32, (1, lanes), 1), shift)
        keep = ((row >= ylo) & (row <= yhi)).astype(F32) * ((col >= xlo) & (col <= xhi)).astype(F32)
        value = silu(summed + bias1[0:1]) * keep
        for a in range(3):
            hid[a, :, pl.ds(c0, lanes)] = value[a : a + length].astype(BF)

        rhs = jnp.concatenate([across[b, pl.ds(r0, 2 * SPAN), :] for b in range(3)], axis=0)
        summed = jnp.dot(band1t[...], rhs, preferred_element_type=F32)
        row = r0 + lax.shift_right_logical(lax.broadcasted_iota(jnp.int32, (lanes, 1), 0), shift)
        col = lax.broadcasted_iota(jnp.int32, (1, wide), 1)
        keep = ((row >= ylo) & (row <= yhi)).astype(F32) * ((col >= xlo) & (col <= xhi)).astype(F32)
        value = silu(summed + bias1t[:, 0:1]) * keep
        for b in range(3):
            hidt[b, pl.ds(c0, lanes), :] = value[:, b : b + length].astype(BF)
        return carry

    lax.fori_loop(0, wide // SPAN, first_layer, 0)

    def second_layer(blk, carry):
        c0 = pl.multiple_of(blk * cols, cols)
        acc = bias2[0:1] + jnp.dot(hid[0, :, pl.ds(c0, depth)], band2[0], preferred_element_type=F32)
        for a in range(1, 3):
            acc = acc + jnp.dot(hid[a, :, pl.ds(c0, depth)], band2[a], preferred_element_type=F32)
        feat[:, pl.ds(c0, cols)] = acc.astype(BF)
        acc = bias2t[:, 0:1] + jnp.dot(band2t[0], hidt[0, pl.ds(c0, depth), :], preferred_element_type=F32)
        for b in range(1, 3):
            acc = acc + jnp.dot(band2t[b], hidt[b, pl.ds(c0, depth), :], preferred_element_type=F32)
        pair = jnp.dot(acc.astype(BF), first[...], preferred_element_type=F32)
        rowwise[0, pl.ds(c0, cols), :] = pair[:, :HALF]
        rowwise[1, pl.ds(c0, cols), :] = pair[:, HALF:]
        return carry

    lax.fori_loop(0, length * channels // cols, second_layer, 0)


def mesh_kernel(
    channels, tissue, coarse, rowwise, left, back, last, flow, nodes_out,
    spec, got, acc, owed, power, node, beside,
    send1, recv1, send2, recv2, send3, recv3,
):
    me = lax.axis_index("sec")
    secs = lax.axis_size("sec")
    row_index, rows_count = lax.axis_index("gy"), lax.axis_size("gy")
    col_index, cols_count = lax.axis_index("gx"), lax.axis_size("gx")
    length = last.shape[1]
    kept = length // 2 + 1
    groups, size = spec.shape[1], spec.shape[2]
    half = size // 2
    peers = [lax.rem(me + r, secs) for r in range(1, secs)]
    targets = [{"sec": peer} for peer in peers]
    targets += [{"gy": lax.rem(row_index + 1, rows_count)}, {"gy": lax.rem(row_index + rows_count - 1, rows_count)}]
    targets += [{"gx": lax.rem(col_index + 1, cols_count)}, {"gx": lax.rem(col_index + cols_count - 1, cols_count)}]
    barrier = pltpu.get_barrier_semaphore()
    for target in targets:
        pl.semaphore_signal(barrier, inc=1, device_id=target, device_id_type=pl.DeviceIdType.MESH)
    pl.semaphore_wait(barrier, len(targets))

    def spread(r, g):
        return pltpu.make_async_remote_copy(
            src_ref=spec.at[peers[r], g],
            dst_ref=got.at[me, g],
            send_sem=send1.at[r, g],
            recv_sem=recv1.at[r, g],
            device_id=targets[r],
            device_id_type=pl.DeviceIdType.MESH,
        )

    wide_lane = lax.broadcasted_iota(jnp.int32, (1, 2 * HALF), 1)
    own_mask = tissue[0].astype(F32)
    own = [coarse[0].astype(F32), coarse[1].astype(F32)]
    facts = jnp.zeros((1, 2 * HALF), F32)
    for place, fact in enumerate([own_mask] + own):
        facts = jnp.where(wide_lane == 3 * kept + place, fact, facts)

    def columns(g, carry):
        halves = []
        for q in range(2):
            packed = None
            for i in range(3):
                c = g * 3 + i
                value = rowwise[q, pl.ds(jnp.minimum(c, channels - 1), length, stride=channels), :]
                value = jnp.concatenate([value, jnp.zeros_like(value)], axis=1)
                if i == 0:
                    packed = value
                else:
                    value = value * (c < channels).astype(F32)
                    packed = packed + pltpu.roll(value, i * kept, 1)
            halves.append(packed.astype(BF))
        out = jnp.dot(left[...], jnp.concatenate(halves, axis=0), preferred_element_type=F32)
        out = (out + facts).astype(BF)
        for q in range(secs):
            spec[q, g] = out[q * size : (q + 1) * size]
        for r in range(secs - 1):
            spread(r, g).start()
        got[me, g] = spec[me, g]
        return carry

    lax.fori_loop(0, groups, columns, 0)
    acc[...] = jnp.zeros_like(acc)

    def multiply(g, carry):
        for r in range(secs - 1):
            spread(r, g).wait()
        values = [got[t, g].astype(F32) for t in range(secs)]
        for s in range(secs):
            for lag in range(1, min(s, LAGS) + 1):
                cur, ear = values[s], values[s - lag]
                acc[s, lag - 1, :half] += ear[:half] * cur[:half] + ear[half:] * cur[half:]
                acc[s, lag - 1, half:] += ear[:half] * cur[half:] - ear[half:] * cur[:half]
        return carry

    lax.fori_loop(0, groups, multiply, 0)
    for s in range(secs):
        for lag in range(LAGS):
            whole = acc[s, lag]
            total = whole[:, :HALF]
            for i in range(1, 3):
                total = total + pltpu.roll(whole, 2 * HALF - i * kept, 1)[:, :HALF]
            owed[s, lag] = total
    returns = [
        pltpu.make_async_remote_copy(
            src_ref=owed.at[peers[r]],
            dst_ref=power.at[me],
            send_sem=send2.at[r],
            recv_sem=recv2.at[r],
            device_id=targets[r],
            device_id_type=pl.DeviceIdType.MESH,
        )
        for r in range(secs - 1)
    ]
    for copy in returns:
        copy.start()
    power[me] = owed[me]

    row = lax.broadcasted_iota(jnp.int32, (length, 1), 0)
    col = lax.broadcasted_iota(jnp.int32, (1, length), 1)
    sign_y = jnp.where(row < length // 2, row, row - length).astype(F32)
    sign_x = jnp.where(col < length // 2, col, col - length).astype(F32)
    place = lax.broadcasted_iota(jnp.int32, flow.shape, 0)
    side = lax.broadcasted_iota(jnp.int32, flow.shape, 1)
    lane = lax.broadcasted_iota(jnp.int32, (1, HALF), 1)

    def pick(values, at):
        return jnp.sum(jnp.where(lane == at, values, 0.0))

    scale = 1.0 / (float(length) ** 3 * channels)
    for copy in returns:
        copy.wait()
    stacked = jnp.concatenate(
        [jnp.concatenate([power[q, lag] for q in range(secs)], axis=0) for lag in range(LAGS)], axis=1
    )
    mixed = jnp.dot(back[...], stacked, precision=lax.Precision.HIGHEST, preferred_element_type=F32)
    result = jnp.zeros(flow.shape, F32)
    pulled = [jnp.float32(0.0), jnp.float32(0.0)]
    weights, goals = [], []
    at = 3 * kept - HALF
    for lag in range(LAGS):
        part = mixed[:, lag * HALF : (lag + 1) * HALF]
        lhs = jnp.concatenate([part[:length], part[length:]], axis=1)
        scores = jnp.dot(lhs, last[...], precision=lax.Precision.HIGHEST, preferred_element_type=F32) * scale
        chances = jnp.exp(scores - jnp.max(scores))
        total = jnp.sum(chances)
        usable = (me > lag).astype(F32)
        peak = [
            usable * (jnp.sum(chances * sign_y) / total),
            usable * (jnp.sum(chances * sign_x) / total),
        ]
        prior = got[lax.rem(me + secs - lag - 1, secs), 0, 0:16, HALF : 2 * HALF].astype(F32)[0:1]
        weight = usable * LAG_WEIGHTS[lag] * own_mask * pick(prior, at)
        goal = []
        for d in range(2):
            result = jnp.where((place == lag) & (side == d), peak[d], result)
            before = pick(prior, at + 1 + d)
            goal.append(peak[d] + own[d] - before)
            pulled[d] = pulled[d] + weight * (before + goal[d] - own[d])
        weights.append(weight)
        goals.append(goal)
    flow[...] = result
    current = jnp.zeros(node.shape, F32)
    for d in range(2):
        current = jnp.where(side == d, own[d] + STEP_SIZE * pulled[d], current)
    node[...] = current
    passes = [
        pltpu.make_async_remote_copy(
            src_ref=node,
            dst_ref=beside.at[k],
            send_sem=send3.at[k],
            recv_sem=recv3.at[k],
            device_id=target,
            device_id_type=pl.DeviceIdType.MESH,
        )
        for k, target in enumerate(targets)
    ]
    for copy in passes:
        copy.start()
    for copy in passes:
        copy.wait()
    pull = jnp.zeros(node.shape, F32)
    for lag in range(LAGS):
        goal = jnp.where(side == 0, goals[lag][0], goals[lag][1])
        pull = pull + weights[lag] * (beside[lag] + goal - current)
    inside = [row_index > 0, row_index < rows_count - 1, col_index > 0, col_index < cols_count - 1]
    plane = jnp.zeros(node.shape, F32)
    for k, here in enumerate(inside):
        plane = plane + here.astype(F32) * (beside[secs - 1 + k] - current)
    nodes_out[...] = current + STEP_SIZE * (pull + PLANE_STIFF * plane)


def body(sections, first_kernel, first_bias, second_kernel, second_bias, coarse, tissue):
    length = sections.shape[-1]
    channels = first_kernel.shape[0]
    secs = lax.axis_size("sec")
    first, left, back, last = make_tables(length, secs)
    wide = length + SPAN
    image = extended(sections, (("gy", 1), ("gx", 2)), 2)[0]
    pad = wide + SPAN + 2 - image.shape[0]
    image = jnp.pad(image, ((0, pad), (0, pad)))
    across = jnp.stack([image[: wide + SPAN, b : b + wide] for b in range(3)])
    turned = image.T
    down = jnp.stack([turned[: wide + SPAN, a : a + wide] for a in range(3)])
    vmem = pl.BlockSpec(memory_space=pltpu.VMEM)
    smem = pl.BlockSpec(memory_space=pltpu.SMEM)
    lanes, cols = SPAN * channels, SPAN // 2 * channels
    depth = 12 * channels
    features, rowwise = pl.pallas_call(
        encode_kernel,
        out_shape=(
            jax.ShapeDtypeStruct((length, length * channels), BF),
            jax.ShapeDtypeStruct((2, length * channels, HALF), F32),
        ),
        in_specs=[vmem] * 7,
        out_specs=(vmem, vmem),
        scratch_shapes=[
            pltpu.VMEM((3, length, wide * channels), BF),
            pltpu.VMEM((3, wide * channels, length), BF),
            pltpu.VMEM((6 * SPAN, lanes), BF),
            pltpu.VMEM((lanes, 6 * SPAN), BF),
            pltpu.VMEM((3, depth, cols), BF),
            pltpu.VMEM((3, cols, depth), BF),
            pltpu.VMEM((8, lanes), F32),
            pltpu.VMEM((lanes, 128), F32),
            pltpu.VMEM((8, cols), F32),
            pltpu.VMEM((cols, 128), F32),
        ],
        compiler_params=pltpu.CompilerParams(vmem_limit_bytes=48 * 1024 * 1024),
        name="encode",
    )(
        across, down, first_kernel, second_kernel, first_bias[None, :], second_bias[None, :],
        jnp.asarray(first, BF),
    )
    size = 2 * length // secs
    groups = (channels + 2) // 3
    others = secs - 1
    dma = pltpu.SemaphoreType.DMA
    peaks, nodes = pl.pallas_call(
        functools.partial(mesh_kernel, channels),
        out_shape=(jax.ShapeDtypeStruct((8, 128), F32), jax.ShapeDtypeStruct((8, 128), F32)),
        in_specs=[smem, smem] + [vmem] * 4,
        out_specs=(vmem, vmem),
        scratch_shapes=[
            pltpu.VMEM((secs, groups, size, 2 * HALF), BF),
            pltpu.VMEM((secs, groups, size, 2 * HALF), BF),
            pltpu.VMEM((secs, LAGS, size, 2 * HALF), F32),
            pltpu.VMEM((secs, LAGS, size, HALF), F32),
            pltpu.VMEM((secs, LAGS, size, HALF), F32),
            pltpu.VMEM((8, 128), F32),
            pltpu.VMEM((others + 4, 8, 128), F32),
            dma((others, groups)),
            dma((others, groups)),
            dma((others,)),
            dma((others,)),
            dma((others + 4,)),
            dma((others + 4,)),
        ],
        compiler_params=pltpu.CompilerParams(
            vmem_limit_bytes=32 * 1024 * 1024, collective_id=0, has_side_effects=True
        ),
        name="mesh",
    )(
        tissue.reshape(1), coarse.reshape(2), rowwise, jnp.asarray(left, BF), jnp.asarray(back), jnp.asarray(last),
    )
    return (
        features.reshape(1, length, features.shape[-1]),
        peaks[:LAGS, :2].reshape(1, LAGS, 2, 1, 1),
        nodes[0, :2].reshape(1, 2, 1, 1),
    )


def solution(mesh):
    in_specs = (P("sec", "gy", "gx"), P(), P(), P(), P(), P("sec", None), P("sec", "gy", "gx"))
    out_specs = (P("sec", "gy", "gx"), P("sec", None, None, "gy", "gx"), P("sec", None, "gy", "gx"))
    return jax.shard_map(body, mesh=mesh, in_specs=in_specs, out_specs=out_specs, check_vma=False)
```

```python
import functools

import jax
import jax.numpy as jnp
import numpy as np
from jax import lax
from jax.experimental import pallas as pl
from jax.experimental.pallas import tpu as pltpu
from jax.sharding import PartitionSpec as P

LAGS = 3

LAG_WEIGHTS = (1.0, 0.5, 0.25)
STEP_SIZE = 0.3
PLANE_STIFF = 0.5
SPAN = 16
HALF = 128
BF = jnp.bfloat16
F32 = jnp.float32


def halo_kernel(image, across, down, strips, landed, ext, send, recv):
    length = image.shape[0]
    tall, wide = across.shape[1], across.shape[2]
    row_index, rows_count = lax.axis_index("gy"), lax.axis_size("gy")
    col_index, cols_count = lax.axis_index("gx"), lax.axis_size("gx")
    routes = [(dy, dx, 0 if dy < 0 else 1) for dy in (-1, 1) for dx in (-1, 0, 1)] + [(0, -1, 2), (0, 1, 3)]
    targets = [
        {
            "gy": lax.rem(row_index + dy + rows_count, rows_count),
            "gx": lax.rem(col_index + dx + cols_count, cols_count),
        }
        for dy, dx, _ in routes
    ]
    barrier = pltpu.get_barrier_semaphore()
    for target in targets:
        pl.semaphore_signal(barrier, inc=1, device_id=target, device_id_type=pl.DeviceIdType.MESH)
    own = image[...].astype(F32)
    turned = jnp.transpose(own)
    strips[0] = image[:SPAN]
    strips[1] = image[length - SPAN :]
    strips[2] = turned[:SPAN].astype(BF)
    strips[3] = turned[length - SPAN :].astype(BF)
    pl.semaphore_wait(barrier, len(targets))
    copies = [
        pltpu.make_async_remote_copy(
            src_ref=strips.at[strip],
            dst_ref=landed.at[k],
            send_sem=send.at[k],
            recv_sem=recv.at[k],
            device_id=targets[k],
            device_id_type=pl.DeviceIdType.MESH,
        )
        for k, (_, _, strip) in enumerate(routes)
    ]
    for copy in copies:
        copy.start()
    ext[...] = jnp.zeros_like(ext)
    ext[2 : length + 2, 2 : length + 2] = own
    for copy in copies:
        copy.wait()
    end = length + 2
    for k, (dy, dx, _) in enumerate(routes):
        here = jnp.logical_and(
            jnp.logical_and(row_index - dy >= 0, row_index - dy < rows_count),
            jnp.logical_and(col_index - dx >= 0, col_index - dx < cols_count),
        ).astype(F32)
        strip = landed[k].astype(F32) * here
        if dy == 0:
            strip = jnp.transpose(strip)
            if dx > 0:
                ext[2:end, 0:2] = strip[:, SPAN - 2 :]
            else:
                ext[2:end, end : end + 2] = strip[:, :2]
            continue
        part = strip[SPAN - 2 :] if dy > 0 else strip[:2]
        r0 = 0 if dy > 0 else end
        if dx == 0:
            ext[r0 : r0 + 2, 2:end] = part
        elif dx > 0:
            ext[r0 : r0 + 2, 0:2] = part[:, length - 2 :]
        else:
            ext[r0 : r0 + 2, end : end + 2] = part[:, :2]
    whole = ext[...]
    turned = jnp.transpose(whole)
    for k in range(3):
        across[k] = whole[:tall, k : k + wide].astype(BF)
        down[k] = turned[:tall, k : k + wide].astype(BF)


def make_tables(length, parts):
    ramp = np.arange(length)
    angle = (ramp[:, None] * ramp[None, :] % length) * (2.0 * np.pi / length)
    cos, sin = np.cos(angle), np.sin(angle)
    kept = length // 2 + 1
    first = np.zeros((length, 2 * HALF))
    first[:, :kept] = cos[:, :kept]
    first[:, HALF : HALF + kept] = sin[:, :kept]
    chunk = length // parts
    left, back = [], []
    for q in range(parts):
        rows = slice(q * chunk, (q + 1) * chunk)
        left += [np.concatenate([cos[rows], -sin[rows]], 1), np.concatenate([-sin[rows], -cos[rows]], 1)]
        back += [np.concatenate([cos[:, rows], sin[:, rows]], 0), np.concatenate([-sin[:, rows], cos[:, rows]], 0)]
    times = np.full((kept, 1), 2.0)
    times[0] = times[-1] = 1.0
    last = np.zeros((2 * HALF, length))
    last[:kept] = times * cos[:kept]
    last[HALF : HALF + kept] = -times * sin[:kept]
    return (
        first.astype(np.float32),
        np.concatenate(left, 0).astype(np.float32),
        np.concatenate(back, 1).astype(np.float32),
        last.astype(np.float32),
    )


def silu(values):
    half = 0.5 * values
    return half + half * jnp.tanh(half)


def tiled_eye(channels, lanes):
    lane = lax.broadcasted_iota(jnp.int32, (channels, lanes), 1)
    row = lax.broadcasted_iota(jnp.int32, (channels, lanes), 0)
    return ((lane & (channels - 1)) == row).astype(F32)


def across_rows(left, right):
    return lax.dot_general(left, right, (((0,), (0,)), ((), ())), preferred_element_type=F32)


def encode_kernel(
    across, down, kernel1, kernel2, bias1_in, bias2_in, first,
    feat, rowwise, hid, hidt, band1, band1t, band2, band2t, bias1, bias1t, bias2, bias2t,
):
    length = feat.shape[0]
    wide = across.shape[-1]
    lanes = band1.shape[1]
    cols = band2.shape[2]
    depth = band2.shape[1]
    channels = lanes // SPAN
    shift = channels.bit_length() - 1
    row_index, col_index = lax.axis_index("gy"), lax.axis_index("gx")
    ylo = jnp.where(row_index == 0, 1, 0)
    yhi = jnp.where(row_index == lax.axis_size("gy") - 1, length, length + 1)
    xlo = jnp.where(col_index == 0, 1, 0)
    xhi = jnp.where(col_index == lax.axis_size("gx") - 1, length, length + 1)

    eye = tiled_eye(channels, lanes)
    eye_bf = eye.astype(BF)
    for source, row_ref, col_ref, width in ((bias1_in, bias1, bias1t, lanes), (bias2_in, bias2, bias2t, cols)):
        spread = jnp.broadcast_to(source[...].astype(F32), (8, channels)).astype(BF)
        row = jnp.dot(spread, eye_bf[:, :width], preferred_element_type=F32)
        row_ref[...] = row
        col_ref[...] = jnp.transpose(jnp.broadcast_to(row[0:1], (128, width)))
    tap1 = across_rows(kernel1[...], eye_bf)
    unit = lax.shift_right_logical(lax.broadcasted_iota(jnp.int32, (2 * SPAN, lanes), 1), shift)
    gap = lax.broadcasted_iota(jnp.int32, (2 * SPAN, lanes), 0) - unit
    for ref, outer, inner in ((band1, 3, 1), (band1t, 1, 3)):
        parts = []
        for p in range(3):
            part = jnp.zeros((2 * SPAN, lanes), F32)
            for q in range(3):
                tap = outer * p + inner * q
                part = jnp.where(gap == q, tap1[tap : tap + 1], part)
            parts.append(part)
        whole = jnp.concatenate(parts, axis=0)
        if outer == 1:
            whole = jnp.transpose(whole)
        ref[...] = whole.astype(BF)
    tap2 = across_rows(kernel2[...], eye_bf[:, :cols])
    unit = lax.shift_right_logical(lax.broadcasted_iota(jnp.int32, (channels, cols), 1), shift)
    for a in range(3):
        for x in range(depth // channels):
            part = jnp.zeros((channels, cols), F32)
            for b in range(3):
                row = (3 * a + b) * channels
                part = jnp.where(unit == x - b, tap2[row : row + channels], part)
            band2[a, x * channels : (x + 1) * channels, :] = part.astype(BF)
    unit = lax.shift_right_logical(lax.broadcasted_iota(jnp.int32, (channels, depth), 1), shift)
    for b in range(3):
        taps = []
        for a in range(3):
            at = (3 * a + b) * channels
            taps.append(jnp.dot(kernel2[:, at : at + channels], eye_bf[:, :depth], preferred_element_type=F32))
        for y in range(cols // channels):
            part = jnp.zeros((channels, depth), F32)
            for a in range(3):
                part = jnp.where(unit == y + a, taps[a], part)
            band2t[b, y * channels : (y + 1) * channels, :] = part.astype(BF)

    def first_layer(blk, carry):
        r0 = pl.multiple_of(blk * SPAN, SPAN)
        c0 = pl.multiple_of(blk * lanes, lanes)
        rhs = jnp.concatenate([down[a, pl.ds(r0, 2 * SPAN), :] for a in range(3)], axis=0)
        summed = across_rows(rhs, band1[...])
        row = lax.broadcasted_iota(jnp.int32, (wide, 1), 0)
        col = r0 + lax.shift_right_logical(lax.broadcasted_iota(jnp.int32, (1, lanes), 1), shift)
        keep = ((row >= ylo) & (row <= yhi)).astype(F32) * ((col >= xlo) & (col <= xhi)).astype(F32)
        value = silu(summed + bias1[0:1]) * keep
        for a in range(3):
            hid[a, :, pl.ds(c0, lanes)] = value[a : a + length].astype(BF)

        rhs = jnp.concatenate([across[b, pl.ds(r0, 2 * SPAN), :] for b in range(3)], axis=0)
        summed = jnp.dot(band1t[...], rhs, preferred_element_type=F32)
        row = r0 + lax.shift_right_logical(lax.broadcasted_iota(jnp.int32, (lanes, 1), 0), shift)
        col = lax.broadcasted_iota(jnp.int32, (1, wide), 1)
        keep = ((row >= ylo) & (row <= yhi)).astype(F32) * ((col >= xlo) & (col <= xhi)).astype(F32)
        value = silu(summed + bias1t[:, 0:1]) * keep
        for b in range(3):
            hidt[b, pl.ds(c0, lanes), :] = value[:, b : b + length].astype(BF)
        return carry

    lax.fori_loop(0, wide // SPAN, first_layer, 0)

    def second_layer(blk, carry):
        c0 = pl.multiple_of(blk * cols, cols)
        acc = bias2[0:1] + jnp.dot(hid[0, :, pl.ds(c0, depth)], band2[0], preferred_element_type=F32)
        for a in range(1, 3):
            acc = acc + jnp.dot(hid[a, :, pl.ds(c0, depth)], band2[a], preferred_element_type=F32)
        feat[:, pl.ds(c0, cols)] = acc.astype(BF)
        acc = bias2t[:, 0:1] + jnp.dot(band2t[0], hidt[0, pl.ds(c0, depth), :], preferred_element_type=F32)
        for b in range(1, 3):
            acc = acc + jnp.dot(band2t[b], hidt[b, pl.ds(c0, depth), :], preferred_element_type=F32)
        pair = jnp.dot(acc.astype(BF), first[...], preferred_element_type=F32)
        rowwise[0, pl.ds(c0, cols), :] = pair[:, :HALF]
        rowwise[1, pl.ds(c0, cols), :] = pair[:, HALF:]
        return carry

    lax.fori_loop(0, length * channels // cols, second_layer, 0, unroll=4)


def mesh_kernel(
    channels, tissue, coarse, rowwise, left, back_far, last_far, flow, nodes_out,
    back, last, spec, got, acc, owed, power, node, beside,
    send1, recv1, send2, recv2, send3, recv3, fetched,
):
    fetches = [
        pltpu.make_async_copy(back_far, back, fetched.at[0]),
        pltpu.make_async_copy(last_far, last, fetched.at[1]),
    ]
    for fetch in fetches:
        fetch.start()
    me = lax.axis_index("sec")
    secs = lax.axis_size("sec")
    row_index, rows_count = lax.axis_index("gy"), lax.axis_size("gy")
    col_index, cols_count = lax.axis_index("gx"), lax.axis_size("gx")
    length = last.shape[1]
    kept = length // 2 + 1
    groups, size = spec.shape[1], spec.shape[2]
    half = size // 2
    peers = [lax.rem(me + r, secs) for r in range(1, secs)]
    targets = [{"sec": peer} for peer in peers]
    targets += [{"gy": lax.rem(row_index + 1, rows_count)}, {"gy": lax.rem(row_index + rows_count - 1, rows_count)}]
    targets += [{"gx": lax.rem(col_index + 1, cols_count)}, {"gx": lax.rem(col_index + cols_count - 1, cols_count)}]
    barrier = pltpu.get_barrier_semaphore()
    for target in targets:
        pl.semaphore_signal(barrier, inc=1, device_id=target, device_id_type=pl.DeviceIdType.MESH)
    pl.semaphore_wait(barrier, len(targets))

    def spread(r, g):
        return pltpu.make_async_remote_copy(
            src_ref=spec.at[peers[r], g],
            dst_ref=got.at[me, g],
            send_sem=send1.at[r, g],
            recv_sem=recv1.at[r, g],
            device_id=targets[r],
            device_id_type=pl.DeviceIdType.MESH,
        )

    wide_lane = lax.broadcasted_iota(jnp.int32, (1, 2 * HALF), 1)
    own_mask = tissue[0].astype(F32)
    own = [coarse[0].astype(F32), coarse[1].astype(F32)]
    facts = jnp.zeros((1, 2 * HALF), F32)
    for place, fact in enumerate([own_mask] + own):
        facts = jnp.where(wide_lane == 3 * kept + place, fact, facts)

    def columns(g, carry):
        halves = []
        for q in range(2):
            packed = None
            for i in range(3):
                c = g * 3 + i
                value = rowwise[q, pl.ds(jnp.minimum(c, channels - 1), length, stride=channels), :]
                value = jnp.concatenate([value, jnp.zeros_like(value)], axis=1)
                if i == 0:
                    packed = value
                else:
                    value = value * (c < channels).astype(F32)
                    packed = packed + pltpu.roll(value, i * kept, 1)
            halves.append(packed.astype(BF))
        out = jnp.dot(left[...], jnp.concatenate(halves, axis=0), preferred_element_type=F32)
        out = (out + facts).astype(BF)
        for q in range(secs):
            spec[q, g] = out[q * size : (q + 1) * size]
        for r in range(secs - 1):
            spread(r, g).start()
        got[me, g] = spec[me, g]
        return carry

    lax.fori_loop(0, groups, columns, 0)
    acc[...] = jnp.zeros_like(acc)

    def multiply(g, carry):
        for r in range(secs - 1):
            spread(r, g).wait()
        values = [got[t, g].astype(F32) for t in range(secs)]
        for s in range(secs):
            for lag in range(1, min(s, LAGS) + 1):
                cur, ear = values[s], values[s - lag]
                acc[s, lag - 1, :half] += ear[:half] * cur[:half] + ear[half:] * cur[half:]
                acc[s, lag - 1, half:] += ear[:half] * cur[half:] - ear[half:] * cur[:half]
        return carry

    lax.fori_loop(0, groups, multiply, 0)
    for s in range(secs):
        for lag in range(LAGS):
            whole = acc[s, lag]
            total = whole[:, :HALF]
            for i in range(1, 3):
                total = total + pltpu.roll(whole, 2 * HALF - i * kept, 1)[:, :HALF]
            owed[s, lag] = total
    returns = [
        pltpu.make_async_remote_copy(
            src_ref=owed.at[peers[r]],
            dst_ref=power.at[me],
            send_sem=send2.at[r],
            recv_sem=recv2.at[r],
            device_id=targets[r],
            device_id_type=pl.DeviceIdType.MESH,
        )
        for r in range(secs - 1)
    ]
    for copy in returns:
        copy.start()
    power[me] = owed[me]

    row = lax.broadcasted_iota(jnp.int32, (length, 1), 0)
    col = lax.broadcasted_iota(jnp.int32, (1, length), 1)
    sign_y = jnp.where(row < length // 2, row, row - length).astype(F32)
    sign_x = jnp.where(col < length // 2, col, col - length).astype(F32)
    place = lax.broadcasted_iota(jnp.int32, flow.shape, 0)
    side = lax.broadcasted_iota(jnp.int32, flow.shape, 1)
    lane = lax.broadcasted_iota(jnp.int32, (1, HALF), 1)

    def pick(values, at):
        return jnp.sum(jnp.where(lane == at, values, 0.0))

    scale = 1.0 / (float(length) ** 3 * channels)
    for copy in returns:
        copy.wait()
    for fetch in fetches:
        fetch.wait()
    stacked = jnp.concatenate(
        [jnp.concatenate([power[q, lag] for q in range(secs)], axis=0) for lag in range(LAGS)], axis=1
    )
    mixed = jnp.dot(back[...], stacked, precision=lax.Precision.HIGHEST, preferred_element_type=F32)
    result = jnp.zeros(flow.shape, F32)
    pulled = [jnp.float32(0.0), jnp.float32(0.0)]
    weights, goals = [], []
    at = 3 * kept - HALF
    for lag in range(LAGS):
        part = mixed[:, lag * HALF : (lag + 1) * HALF]
        lhs = jnp.concatenate([part[:length], part[length:]], axis=1)
        scores = jnp.dot(lhs, last[...], precision=lax.Precision.HIGHEST, preferred_element_type=F32) * scale
        chances = jnp.exp(scores - jnp.max(scores))
        total = jnp.sum(chances)
        usable = (me > lag).astype(F32)
        peak = [
            usable * (jnp.sum(chances * sign_y) / total),
            usable * (jnp.sum(chances * sign_x) / total),
        ]
        prior = got[lax.rem(me + secs - lag - 1, secs), 0, 0:16, HALF : 2 * HALF].astype(F32)[0:1]
        weight = usable * LAG_WEIGHTS[lag] * own_mask * pick(prior, at)
        goal = []
        for d in range(2):
            result = jnp.where((place == lag) & (side == d), peak[d], result)
            before = pick(prior, at + 1 + d)
            goal.append(peak[d] + own[d] - before)
            pulled[d] = pulled[d] + weight * (before + goal[d] - own[d])
        weights.append(weight)
        goals.append(goal)
    flow[...] = result
    current = jnp.zeros(node.shape, F32)
    for d in range(2):
        current = jnp.where(side == d, own[d] + STEP_SIZE * pulled[d], current)
    node[...] = current
    passes = [
        pltpu.make_async_remote_copy(
            src_ref=node,
            dst_ref=beside.at[k],
            send_sem=send3.at[k],
            recv_sem=recv3.at[k],
            device_id=target,
            device_id_type=pl.DeviceIdType.MESH,
        )
        for k, target in enumerate(targets)
    ]
    for copy in passes:
        copy.start()
    for copy in passes:
        copy.wait()
    pull = jnp.zeros(node.shape, F32)
    for lag in range(LAGS):
        goal = jnp.where(side == 0, goals[lag][0], goals[lag][1])
        pull = pull + weights[lag] * (beside[lag] + goal - current)
    inside = [row_index > 0, row_index < rows_count - 1, col_index > 0, col_index < cols_count - 1]
    plane = jnp.zeros(node.shape, F32)
    for k, here in enumerate(inside):
        plane = plane + here.astype(F32) * (beside[secs - 1 + k] - current)
    nodes_out[...] = current + STEP_SIZE * (pull + PLANE_STIFF * plane)


def body(sections, first_kernel, first_bias, second_kernel, second_bias, coarse, tissue):
    length = sections.shape[-1]
    channels = first_kernel.shape[0]
    secs = lax.axis_size("sec")
    first, left, back, last = make_tables(length, secs)
    wide = length + SPAN
    vmem = pl.BlockSpec(memory_space=pltpu.VMEM)
    dma = pltpu.SemaphoreType.DMA
    tall = wide + SPAN
    frame = jax.ShapeDtypeStruct((3, tall, wide), BF)
    across, down = pl.pallas_call(
        halo_kernel,
        out_shape=(frame, frame),
        in_specs=[vmem],
        out_specs=(vmem, vmem),
        scratch_shapes=[
            pltpu.VMEM((4, SPAN, length), BF),
            pltpu.VMEM((8, SPAN, length), BF),
            pltpu.VMEM((256, 256), F32),
            dma((8,)),
            dma((8,)),
        ],
        compiler_params=pltpu.CompilerParams(
            vmem_limit_bytes=16 * 1024 * 1024, collective_id=1, has_side_effects=True
        ),
        name="halo",
    )(sections[0])
    smem = pl.BlockSpec(memory_space=pltpu.SMEM)
    lanes, cols = SPAN * channels, SPAN // 2 * channels
    depth = 12 * channels
    features, rowwise = pl.pallas_call(
        encode_kernel,
        out_shape=(
            jax.ShapeDtypeStruct((length, length * channels), BF),
            jax.ShapeDtypeStruct((2, length * channels, HALF), F32),
        ),
        in_specs=[vmem] * 7,
        out_specs=(vmem, vmem),
        scratch_shapes=[
            pltpu.VMEM((3, length, wide * channels), BF),
            pltpu.VMEM((3, wide * channels, length), BF),
            pltpu.VMEM((6 * SPAN, lanes), BF),
            pltpu.VMEM((lanes, 6 * SPAN), BF),
            pltpu.VMEM((3, depth, cols), BF),
            pltpu.VMEM((3, cols, depth), BF),
            pltpu.VMEM((8, lanes), F32),
            pltpu.VMEM((lanes, 128), F32),
            pltpu.VMEM((8, cols), F32),
            pltpu.VMEM((cols, 128), F32),
        ],
        compiler_params=pltpu.CompilerParams(vmem_limit_bytes=48 * 1024 * 1024),
        name="encode",
    )(
        across, down, first_kernel, second_kernel, first_bias[None, :], second_bias[None, :],
        jnp.asarray(first, BF),
    )
    size = 2 * length // secs
    groups = (channels + 2) // 3
    others = secs - 1
    peaks, nodes = pl.pallas_call(
        functools.partial(mesh_kernel, channels),
        out_shape=(jax.ShapeDtypeStruct((8, 128), F32), jax.ShapeDtypeStruct((8, 128), F32)),
        in_specs=[smem, smem] + [vmem] * 2 + [pl.BlockSpec(memory_space=pltpu.HBM)] * 2,
        out_specs=(vmem, vmem),
        scratch_shapes=[
            pltpu.VMEM(back.shape, F32),
            pltpu.VMEM(last.shape, F32),
            pltpu.VMEM((secs, groups, size, 2 * HALF), BF),
            pltpu.VMEM((secs, groups, size, 2 * HALF), BF),
            pltpu.VMEM((secs, LAGS, size, 2 * HALF), F32),
            pltpu.VMEM((secs, LAGS, size, HALF), F32),
            pltpu.VMEM((secs, LAGS, size, HALF), F32),
            pltpu.VMEM((8, 128), F32),
            pltpu.VMEM((others + 4, 8, 128), F32),
            dma((others, groups)),
            dma((others, groups)),
            dma((others,)),
            dma((others,)),
            dma((others + 4,)),
            dma((others + 4,)),
            dma((2,)),
        ],
        compiler_params=pltpu.CompilerParams(
            vmem_limit_bytes=32 * 1024 * 1024, collective_id=0, has_side_effects=True
        ),
        name="mesh",
    )(
        tissue.reshape(1), coarse.reshape(2), rowwise, jnp.asarray(left, BF), jnp.asarray(back), jnp.asarray(last),
    )
    return (
        features.reshape(1, length, features.shape[-1]),
        peaks[:LAGS, :2].reshape(1, LAGS, 2, 1, 1),
        nodes[0, :2].reshape(1, 2, 1, 1),
    )


def solution(mesh):
    in_specs = (P("sec", "gy", "gx"), P(), P(), P(), P(), P("sec", None), P("sec", "gy", "gx"))
    out_specs = (P("sec", "gy", "gx"), P("sec", None, None, "gy", "gx"), P("sec", None, "gy", "gx"))
    return jax.shard_map(body, mesh=mesh, in_specs=in_specs, out_specs=out_specs, check_vma=False)
```

```python
import functools

import jax
import jax.numpy as jnp
import numpy as np
from jax import lax
from jax.experimental import pallas as pl
from jax.experimental.pallas import tpu as pltpu
from jax.sharding import PartitionSpec as P

LAGS = 3

LAG_WEIGHTS = (1.0, 0.5, 0.25)
STEP_SIZE = 0.3
PLANE_STIFF = 0.5
SPAN = 16
HALF = 128
BF = jnp.bfloat16
F32 = jnp.float32


def halo_kernel(image, across, down, strips, landed, ext, send, recv):
    length = image.shape[0]
    tall, wide = across.shape[1], across.shape[2]
    row_index, rows_count = lax.axis_index("gy"), lax.axis_size("gy")
    col_index, cols_count = lax.axis_index("gx"), lax.axis_size("gx")
    routes = [(dy, dx, 0 if dy < 0 else 1) for dy in (-1, 1) for dx in (-1, 0, 1)] + [(0, -1, 2), (0, 1, 3)]
    targets = [
        {
            "gy": lax.rem(row_index + dy + rows_count, rows_count),
            "gx": lax.rem(col_index + dx + cols_count, cols_count),
        }
        for dy, dx, _ in routes
    ]
    barrier = pltpu.get_barrier_semaphore()
    for target in targets:
        pl.semaphore_signal(barrier, inc=1, device_id=target, device_id_type=pl.DeviceIdType.MESH)
    own = image[...].astype(F32)
    turned = jnp.transpose(own)
    strips[0] = image[:SPAN]
    strips[1] = image[length - SPAN :]
    strips[2] = turned[:SPAN].astype(BF)
    strips[3] = turned[length - SPAN :].astype(BF)
    pl.semaphore_wait(barrier, len(targets))
    copies = [
        pltpu.make_async_remote_copy(
            src_ref=strips.at[strip],
            dst_ref=landed.at[k],
            send_sem=send.at[k],
            recv_sem=recv.at[k],
            device_id=targets[k],
            device_id_type=pl.DeviceIdType.MESH,
        )
        for k, (_, _, strip) in enumerate(routes)
    ]
    for copy in copies:
        copy.start()
    ext[...] = jnp.zeros_like(ext)
    ext[2 : length + 2, 2 : length + 2] = own
    for copy in copies:
        copy.wait()
    end = length + 2
    for k, (dy, dx, _) in enumerate(routes):
        here = jnp.logical_and(
            jnp.logical_and(row_index - dy >= 0, row_index - dy < rows_count),
            jnp.logical_and(col_index - dx >= 0, col_index - dx < cols_count),
        ).astype(F32)
        strip = landed[k].astype(F32) * here
        if dy == 0:
            strip = jnp.transpose(strip)
            if dx > 0:
                ext[2:end, 0:2] = strip[:, SPAN - 2 :]
            else:
                ext[2:end, end : end + 2] = strip[:, :2]
            continue
        part = strip[SPAN - 2 :] if dy > 0 else strip[:2]
        r0 = 0 if dy > 0 else end
        if dx == 0:
            ext[r0 : r0 + 2, 2:end] = part
        elif dx > 0:
            ext[r0 : r0 + 2, 0:2] = part[:, length - 2 :]
        else:
            ext[r0 : r0 + 2, end : end + 2] = part[:, :2]
    whole = ext[...]
    turned = jnp.transpose(whole)
    for k in range(3):
        across[k] = whole[:tall, k : k + wide].astype(BF)
        down[k] = turned[:tall, k : k + wide].astype(BF)


def make_tables(length, parts):
    ramp = np.arange(length)
    angle = (ramp[:, None] * ramp[None, :] % length) * (2.0 * np.pi / length)
    cos, sin = np.cos(angle), np.sin(angle)
    kept = length // 2 + 1
    first = np.zeros((length, 2 * HALF))
    first[:, :kept] = cos[:, :kept]
    first[:, HALF : HALF + kept] = sin[:, :kept]
    chunk = length // parts
    left, back = [], []
    for q in range(parts):
        rows = slice(q * chunk, (q + 1) * chunk)
        left += [np.concatenate([cos[rows], -sin[rows]], 1), np.concatenate([-sin[rows], -cos[rows]], 1)]
        back += [np.concatenate([cos[:, rows], sin[:, rows]], 0), np.concatenate([-sin[:, rows], cos[:, rows]], 0)]
    times = np.full((kept, 1), 2.0)
    times[0] = times[-1] = 1.0
    last = np.zeros((2 * HALF, length))
    last[:kept] = times * cos[:kept]
    last[HALF : HALF + kept] = -times * sin[:kept]
    return (
        first.astype(np.float32),
        np.concatenate(left, 0).astype(np.float32),
        np.concatenate(back, 1).astype(np.float32),
        last.astype(np.float32),
    )


def silu(values):
    half = 0.5 * values
    return half + half * jnp.tanh(half)


def tiled_eye(channels, lanes):
    lane = lax.broadcasted_iota(jnp.int32, (channels, lanes), 1)
    row = lax.broadcasted_iota(jnp.int32, (channels, lanes), 0)
    return ((lane & (channels - 1)) == row).astype(F32)


def across_rows(left, right):
    return lax.dot_general(left, right, (((0,), (0,)), ((), ())), preferred_element_type=F32)


def encode_kernel(
    across, down, kernel1, kernel2, bias1_in, bias2_in, first,
    feat, rowwise, hid, hidt, band1, band1t, band2, band2t, bias1, bias1t, bias2, bias2t,
):
    length = feat.shape[0]
    wide = across.shape[-1]
    lanes = band1.shape[1]
    cols = band2.shape[2]
    depth = band2.shape[1]
    channels = lanes // SPAN
    shift = channels.bit_length() - 1
    row_index, col_index = lax.axis_index("gy"), lax.axis_index("gx")
    ylo = jnp.where(row_index == 0, 1, 0)
    yhi = jnp.where(row_index == lax.axis_size("gy") - 1, length, length + 1)
    xlo = jnp.where(col_index == 0, 1, 0)
    xhi = jnp.where(col_index == lax.axis_size("gx") - 1, length, length + 1)

    eye = tiled_eye(channels, lanes)
    eye_bf = eye.astype(BF)
    for source, row_ref, col_ref, width in ((bias1_in, bias1, bias1t, lanes), (bias2_in, bias2, bias2t, cols)):
        spread = jnp.broadcast_to(source[...].astype(F32), (8, channels)).astype(BF)
        row = jnp.dot(spread, eye_bf[:, :width], preferred_element_type=F32)
        row_ref[...] = row
        col_ref[...] = jnp.transpose(jnp.broadcast_to(row[0:1], (128, width)))
    tap1 = across_rows(kernel1[...], eye_bf)
    unit = lax.shift_right_logical(lax.broadcasted_iota(jnp.int32, (2 * SPAN, lanes), 1), shift)
    gap = lax.broadcasted_iota(jnp.int32, (2 * SPAN, lanes), 0) - unit
    for ref, outer, inner in ((band1, 3, 1), (band1t, 1, 3)):
        parts = []
        for p in range(3):
            part = jnp.zeros((2 * SPAN, lanes), F32)
            for q in range(3):
                tap = outer * p + inner * q
                part = jnp.where(gap == q, tap1[tap : tap + 1], part)
            parts.append(part)
        whole = jnp.concatenate(parts, axis=0)
        if outer == 1:
            whole = jnp.transpose(whole)
        ref[...] = whole.astype(BF)
    tap2 = across_rows(kernel2[...], eye_bf[:, :cols])
    unit = lax.shift_right_logical(lax.broadcasted_iota(jnp.int32, (channels, cols), 1), shift)
    for a in range(3):
        for x in range(depth // channels):
            part = jnp.zeros((channels, cols), F32)
            for b in range(3):
                row = (3 * a + b) * channels
                part = jnp.where(unit == x - b, tap2[row : row + channels], part)
            band2[a, x * channels : (x + 1) * channels, :] = part.astype(BF)
    unit = lax.shift_right_logical(lax.broadcasted_iota(jnp.int32, (channels, depth), 1), shift)
    for b in range(3):
        taps = []
        for a in range(3):
            at = (3 * a + b) * channels
            taps.append(jnp.dot(kernel2[:, at : at + channels], eye_bf[:, :depth], preferred_element_type=F32))
        for y in range(cols // channels):
            part = jnp.zeros((channels, depth), F32)
            for a in range(3):
                part = jnp.where(unit == y + a, taps[a], part)
            band2t[b, y * channels : (y + 1) * channels, :] = part.astype(BF)

    def first_layer(blk, carry):
        r0 = pl.multiple_of(blk * SPAN, SPAN)
        c0 = pl.multiple_of(blk * lanes, lanes)
        rhs = jnp.concatenate([down[a, pl.ds(r0, 2 * SPAN), :] for a in range(3)], axis=0)
        summed = across_rows(rhs, band1[...])
        row = lax.broadcasted_iota(jnp.int32, (wide, 1), 0)
        col = r0 + lax.shift_right_logical(lax.broadcasted_iota(jnp.int32, (1, lanes), 1), shift)
        keep = ((row >= ylo) & (row <= yhi)).astype(F32) * ((col >= xlo) & (col <= xhi)).astype(F32)
        value = silu(summed + bias1[0:1]) * keep
        for a in range(3):
            hid[a, :, pl.ds(c0, lanes)] = value[a : a + length].astype(BF)

        rhs = jnp.concatenate([across[b, pl.ds(r0, 2 * SPAN), :] for b in range(3)], axis=0)
        summed = jnp.dot(band1t[...], rhs, preferred_element_type=F32)
        row = r0 + lax.shift_right_logical(lax.broadcasted_iota(jnp.int32, (lanes, 1), 0), shift)
        col = lax.broadcasted_iota(jnp.int32, (1, wide), 1)
        keep = ((row >= ylo) & (row <= yhi)).astype(F32) * ((col >= xlo) & (col <= xhi)).astype(F32)
        value = silu(summed + bias1t[:, 0:1]) * keep
        for b in range(3):
            hidt[b, pl.ds(c0, lanes), :] = value[:, b : b + length].astype(BF)
        return carry

    lax.fori_loop(0, wide // SPAN, first_layer, 0)

    def second_layer(blk, carry):
        c0 = pl.multiple_of(blk * cols, cols)
        window = jnp.concatenate([hid[a, :, pl.ds(c0, depth)] for a in range(3)], axis=1)
        acc = bias2[0:1] + jnp.dot(window, band2[...].reshape(3 * depth, cols), preferred_element_type=F32)
        feat[:, pl.ds(c0, cols)] = acc.astype(BF)
        window = jnp.concatenate([hidt[b, pl.ds(c0, depth), :] for b in range(3)], axis=0)
        band = jnp.concatenate([band2t[b] for b in range(3)], axis=1)
        acc = bias2t[:, 0:1] + jnp.dot(band, window, preferred_element_type=F32)
        pair = jnp.dot(acc.astype(BF), first[...], preferred_element_type=F32)
        rowwise[0, pl.ds(c0, cols), :] = pair[:, :HALF]
        rowwise[1, pl.ds(c0, cols), :] = pair[:, HALF:]
        return carry

    lax.fori_loop(0, length * channels // cols, second_layer, 0, unroll=4)


def mesh_kernel(
    channels, tissue, coarse, rowwise, tables, flow, nodes_out,
    left, spec, got, acc, owed, power, node, beside,
    send1, recv1, send2, recv2, send3, recv3,
):
    me = lax.axis_index("sec")
    secs = lax.axis_size("sec")
    row_index, rows_count = lax.axis_index("gy"), lax.axis_size("gy")
    col_index, cols_count = lax.axis_index("gx"), lax.axis_size("gx")
    length = rowwise.shape[1] // channels
    kept = length // 2 + 1
    double = 2 * length
    apart = -(-double // HALF) * HALF
    groups, size = spec.shape[1], spec.shape[2]
    half = size // 2
    peers = [lax.rem(me + r, secs) for r in range(1, secs)]
    targets = [{"sec": peer} for peer in peers]
    targets += [{"gy": lax.rem(row_index + 1, rows_count)}, {"gy": lax.rem(row_index + rows_count - 1, rows_count)}]
    targets += [{"gx": lax.rem(col_index + 1, cols_count)}, {"gx": lax.rem(col_index + cols_count - 1, cols_count)}]
    barrier = pltpu.get_barrier_semaphore()
    for target in targets:
        pl.semaphore_signal(barrier, inc=1, device_id=target, device_id_type=pl.DeviceIdType.MESH)
    left[...] = tables[:, :double].astype(BF)
    pl.semaphore_wait(barrier, len(targets))

    def spread(r, g):
        return pltpu.make_async_remote_copy(
            src_ref=spec.at[peers[r], g],
            dst_ref=got.at[me, g],
            send_sem=send1.at[r, g],
            recv_sem=recv1.at[r, g],
            device_id=targets[r],
            device_id_type=pl.DeviceIdType.MESH,
        )

    wide_lane = lax.broadcasted_iota(jnp.int32, (1, 2 * HALF), 1)
    own_mask = tissue[0].astype(F32)
    own = [coarse[0].astype(F32), coarse[1].astype(F32)]
    facts = jnp.zeros((1, 2 * HALF), F32)
    for place, fact in enumerate([own_mask] + own):
        facts = jnp.where(wide_lane == 3 * kept + place, fact, facts)

    def columns(g, carry):
        halves = []
        for q in range(2):
            packed = None
            for i in range(3):
                c = g * 3 + i
                value = rowwise[q, pl.ds(jnp.minimum(c, channels - 1), length, stride=channels), :]
                value = jnp.concatenate([value, jnp.zeros_like(value)], axis=1)
                if i == 0:
                    packed = value
                else:
                    value = value * (c < channels).astype(F32)
                    packed = packed + pltpu.roll(value, i * kept, 1)
            halves.append(packed.astype(BF))
        out = jnp.dot(left[...], jnp.concatenate(halves, axis=0), preferred_element_type=F32)
        out = (out + facts).astype(BF)
        for q in range(secs):
            spec[q, g] = out[q * size : (q + 1) * size]
        for r in range(secs - 1):
            spread(r, g).start()
        got[me, g] = spec[me, g]
        return carry

    lax.fori_loop(0, groups, columns, 0)
    acc[...] = jnp.zeros_like(acc)

    def multiply(g, carry):
        for r in range(secs - 1):
            spread(r, g).wait()
        values = [got[t, g].astype(F32) for t in range(secs)]
        for s in range(secs):
            for lag in range(1, min(s, LAGS) + 1):
                cur, ear = values[s], values[s - lag]
                acc[s, lag - 1, :half] += ear[:half] * cur[:half] + ear[half:] * cur[half:]
                acc[s, lag - 1, half:] += ear[:half] * cur[half:] - ear[half:] * cur[:half]
        return carry

    lax.fori_loop(0, groups, multiply, 0)
    for s in range(secs):
        for lag in range(LAGS):
            whole = acc[s, lag]
            total = whole[:, :HALF]
            for i in range(1, 3):
                total = total + pltpu.roll(whole, 2 * HALF - i * kept, 1)[:, :HALF]
            owed[s, lag] = total
    returns = [
        pltpu.make_async_remote_copy(
            src_ref=owed.at[peers[r]],
            dst_ref=power.at[me],
            send_sem=send2.at[r],
            recv_sem=recv2.at[r],
            device_id=targets[r],
            device_id_type=pl.DeviceIdType.MESH,
        )
        for r in range(secs - 1)
    ]
    for copy in returns:
        copy.start()
    power[me] = owed[me]

    row = lax.broadcasted_iota(jnp.int32, (length, 1), 0)
    col = lax.broadcasted_iota(jnp.int32, (1, length), 1)
    sign_y = jnp.where(row < length // 2, row, row - length).astype(F32)
    sign_x = jnp.where(col < length // 2, col, col - length).astype(F32)
    place = lax.broadcasted_iota(jnp.int32, flow.shape, 0)
    side = lax.broadcasted_iota(jnp.int32, flow.shape, 1)
    lane = lax.broadcasted_iota(jnp.int32, (1, HALF), 1)

    def pick(values, at):
        return jnp.sum(jnp.where(lane == at, values, 0.0))

    scale = 1.0 / (float(length) ** 3 * channels)
    for copy in returns:
        copy.wait()
    last = tables[: 2 * HALF, 2 * apart : 2 * apart + length]
    stacked = jnp.concatenate(
        [jnp.concatenate([power[q, lag] for q in range(secs)], axis=0) for lag in range(LAGS)], axis=1
    )
    mixed = jnp.dot(tables[:, apart : apart + double], stacked, precision=lax.Precision.HIGHEST, preferred_element_type=F32)
    result = jnp.zeros(flow.shape, F32)
    pulled = [jnp.float32(0.0), jnp.float32(0.0)]
    weights, goals = [], []
    at = 3 * kept - HALF
    for lag in range(LAGS):
        part = mixed[:, lag * HALF : (lag + 1) * HALF]
        lhs = jnp.concatenate([part[:length], part[length:]], axis=1)
        scores = jnp.dot(lhs, last, precision=lax.Precision.HIGHEST, preferred_element_type=F32) * scale
        chances = jnp.exp(scores - jnp.max(scores))
        total = jnp.sum(chances)
        usable = (me > lag).astype(F32)
        peak = [
            usable * (jnp.sum(chances * sign_y) / total),
            usable * (jnp.sum(chances * sign_x) / total),
        ]
        prior = got[lax.rem(me + secs - lag - 1, secs), 0, 0:16, HALF : 2 * HALF].astype(F32)[0:1]
        weight = usable * LAG_WEIGHTS[lag] * own_mask * pick(prior, at)
        goal = []
        for d in range(2):
            result = jnp.where((place == lag) & (side == d), peak[d], result)
            before = pick(prior, at + 1 + d)
            goal.append(peak[d] + own[d] - before)
            pulled[d] = pulled[d] + weight * (before + goal[d] - own[d])
        weights.append(weight)
        goals.append(goal)
    flow[...] = result
    current = jnp.zeros(node.shape, F32)
    for d in range(2):
        current = jnp.where(side == d, own[d] + STEP_SIZE * pulled[d], current)
    node[...] = current
    passes = [
        pltpu.make_async_remote_copy(
            src_ref=node,
            dst_ref=beside.at[k],
            send_sem=send3.at[k],
            recv_sem=recv3.at[k],
            device_id=target,
            device_id_type=pl.DeviceIdType.MESH,
        )
        for k, target in enumerate(targets)
    ]
    for copy in passes:
        copy.start()
    for copy in passes:
        copy.wait()
    pull = jnp.zeros(node.shape, F32)
    for lag in range(LAGS):
        goal = jnp.where(side == 0, goals[lag][0], goals[lag][1])
        pull = pull + weights[lag] * (beside[lag] + goal - current)
    inside = [row_index > 0, row_index < rows_count - 1, col_index > 0, col_index < cols_count - 1]
    plane = jnp.zeros(node.shape, F32)
    for k, here in enumerate(inside):
        plane = plane + here.astype(F32) * (beside[secs - 1 + k] - current)
    nodes_out[...] = current + STEP_SIZE * (pull + PLANE_STIFF * plane)


def body(sections, first_kernel, first_bias, second_kernel, second_bias, coarse, tissue):
    length = sections.shape[-1]
    channels = first_kernel.shape[0]
    secs = lax.axis_size("sec")
    first, left, back, last = make_tables(length, secs)
    wide = length + SPAN
    vmem = pl.BlockSpec(memory_space=pltpu.VMEM)
    dma = pltpu.SemaphoreType.DMA
    tall = wide + SPAN
    frame = jax.ShapeDtypeStruct((3, tall, wide), BF)
    across, down = pl.pallas_call(
        halo_kernel,
        out_shape=(frame, frame),
        in_specs=[vmem],
        out_specs=(vmem, vmem),
        scratch_shapes=[
            pltpu.VMEM((4, SPAN, length), BF),
            pltpu.VMEM((8, SPAN, length), BF),
            pltpu.VMEM((256, 256), F32),
            dma((8,)),
            dma((8,)),
        ],
        compiler_params=pltpu.CompilerParams(
            vmem_limit_bytes=8 * 1024 * 1024, collective_id=1, has_side_effects=True
        ),
        name="halo",
    )(sections[0])
    smem = pl.BlockSpec(memory_space=pltpu.SMEM)
    lanes, cols = SPAN * channels, SPAN // 2 * channels
    depth = 12 * channels
    features, rowwise = pl.pallas_call(
        encode_kernel,
        out_shape=(
            jax.ShapeDtypeStruct((length, length * channels), BF),
            jax.ShapeDtypeStruct((2, length * channels, HALF), F32),
        ),
        in_specs=[vmem] * 7,
        out_specs=(vmem, vmem),
        scratch_shapes=[
            pltpu.VMEM((3, length, wide * channels), BF),
            pltpu.VMEM((3, wide * channels, length), BF),
            pltpu.VMEM((6 * SPAN, lanes), BF),
            pltpu.VMEM((lanes, 6 * SPAN), BF),
            pltpu.VMEM((3, depth, cols), BF),
            pltpu.VMEM((3, cols, depth), BF),
            pltpu.VMEM((8, lanes), F32),
            pltpu.VMEM((lanes, 128), F32),
            pltpu.VMEM((8, cols), F32),
            pltpu.VMEM((cols, 128), F32),
        ],
        compiler_params=pltpu.CompilerParams(vmem_limit_bytes=26 * 1024 * 1024),
        name="encode",
    )(
        across, down, first_kernel, second_kernel, first_bias[None, :], second_bias[None, :],
        jnp.asarray(first, BF),
    )
    size = 2 * length // secs
    apart = -(-2 * length // HALF) * HALF
    joined = np.zeros((2 * length, 2 * apart + 2 * HALF), np.float32)
    joined[:, : 2 * length] = left
    joined[:, apart : apart + 2 * length] = back
    joined[: 2 * HALF, 2 * apart : 2 * apart + length] = last
    groups = (channels + 2) // 3
    others = secs - 1
    peaks, nodes = pl.pallas_call(
        functools.partial(mesh_kernel, channels),
        out_shape=(jax.ShapeDtypeStruct((8, 128), F32), jax.ShapeDtypeStruct((8, 128), F32)),
        in_specs=[smem, smem] + [vmem] * 2,
        out_specs=(vmem, vmem),
        scratch_shapes=[
            pltpu.VMEM(left.shape, BF),
            pltpu.VMEM((secs, groups, size, 2 * HALF), BF),
            pltpu.VMEM((secs, groups, size, 2 * HALF), BF),
            pltpu.VMEM((secs, LAGS, size, 2 * HALF), F32),
            pltpu.VMEM((secs, LAGS, size, HALF), F32),
            pltpu.VMEM((secs, LAGS, size, HALF), F32),
            pltpu.VMEM((8, 128), F32),
            pltpu.VMEM((others + 4, 8, 128), F32),
            dma((others, groups)),
            dma((others, groups)),
            dma((others,)),
            dma((others,)),
            dma((others + 4,)),
            dma((others + 4,)),
        ],
        compiler_params=pltpu.CompilerParams(
            vmem_limit_bytes=18 * 1024 * 1024, collective_id=0, has_side_effects=True
        ),
        name="mesh",
    )(
        tissue.reshape(1), coarse.reshape(2), rowwise, jnp.asarray(joined),
    )
    return (
        features.reshape(1, length, features.shape[-1]),
        peaks[:LAGS, :2].reshape(1, LAGS, 2, 1, 1),
        nodes[0, :2].reshape(1, 2, 1, 1),
    )


def solution(mesh):
    in_specs = (P("sec", "gy", "gx"), P(), P(), P(), P(), P("sec", None), P("sec", "gy", "gx"))
    out_specs = (P("sec", "gy", "gx"), P("sec", None, None, "gy", "gx"), P("sec", None, "gy", "gx"))
    return jax.shard_map(body, mesh=mesh, in_specs=in_specs, out_specs=out_specs, check_vma=False)
```

```python
import functools

import jax
import jax.numpy as jnp
import numpy as np
from jax import lax
from jax.experimental import pallas as pl
from jax.experimental.pallas import tpu as pltpu
from jax.sharding import PartitionSpec as P

LAGS = 3

LAG_WEIGHTS = (1.0, 0.5, 0.25)
STEP_SIZE = 0.3
PLANE_STIFF = 0.5
SPAN = 16
HALF = 128
BF = jnp.bfloat16
F32 = jnp.float32


def halo_kernel(image, across, down, strips, landed, ext, send, recv):
    length = image.shape[0]
    tall, wide = across.shape[1], across.shape[2]
    row_index, rows_count = lax.axis_index("gy"), lax.axis_size("gy")
    col_index, cols_count = lax.axis_index("gx"), lax.axis_size("gx")
    routes = [(dy, dx, 0 if dy < 0 else 1) for dy in (-1, 1) for dx in (-1, 0, 1)] + [(0, -1, 2), (0, 1, 3)]
    targets = [
        {
            "gy": lax.rem(row_index + dy + rows_count, rows_count),
            "gx": lax.rem(col_index + dx + cols_count, cols_count),
        }
        for dy, dx, _ in routes
    ]
    barrier = pltpu.get_barrier_semaphore()
    for target in targets:
        pl.semaphore_signal(barrier, inc=1, device_id=target, device_id_type=pl.DeviceIdType.MESH)
    own = image[...].astype(F32)
    turned = jnp.transpose(own)
    strips[0] = image[:SPAN]
    strips[1] = image[length - SPAN :]
    strips[2] = turned[:SPAN].astype(BF)
    strips[3] = turned[length - SPAN :].astype(BF)
    pl.semaphore_wait(barrier, len(targets))
    copies = [
        pltpu.make_async_remote_copy(
            src_ref=strips.at[strip],
            dst_ref=landed.at[k],
            send_sem=send.at[k],
            recv_sem=recv.at[k],
            device_id=targets[k],
            device_id_type=pl.DeviceIdType.MESH,
        )
        for k, (_, _, strip) in enumerate(routes)
    ]
    for copy in copies:
        copy.start()
    ext[...] = jnp.zeros_like(ext)
    ext[2 : length + 2, 2 : length + 2] = own
    for copy in copies:
        copy.wait()
    end = length + 2
    for k, (dy, dx, _) in enumerate(routes):
        here = jnp.logical_and(
            jnp.logical_and(row_index - dy >= 0, row_index - dy < rows_count),
            jnp.logical_and(col_index - dx >= 0, col_index - dx < cols_count),
        ).astype(F32)
        strip = landed[k].astype(F32) * here
        if dy == 0:
            strip = jnp.transpose(strip)
            if dx > 0:
                ext[2:end, 0:2] = strip[:, SPAN - 2 :]
            else:
                ext[2:end, end : end + 2] = strip[:, :2]
            continue
        part = strip[SPAN - 2 :] if dy > 0 else strip[:2]
        r0 = 0 if dy > 0 else end
        if dx == 0:
            ext[r0 : r0 + 2, 2:end] = part
        elif dx > 0:
            ext[r0 : r0 + 2, 0:2] = part[:, length - 2 :]
        else:
            ext[r0 : r0 + 2, end : end + 2] = part[:, :2]
    whole = ext[...]
    turned = jnp.transpose(whole)
    for k in range(3):
        across[k] = whole[:tall, k : k + wide].astype(BF)
        down[k] = turned[:tall, k : k + wide].astype(BF)


def make_tables(length, parts):
    ramp = np.arange(length)
    angle = (ramp[:, None] * ramp[None, :] % length) * (2.0 * np.pi / length)
    cos, sin = np.cos(angle), np.sin(angle)
    kept = length // 2 + 1
    first = np.zeros((length, 2 * HALF))
    first[:, :kept] = cos[:, :kept]
    first[:, HALF : HALF + kept] = sin[:, :kept]
    chunk = length // parts
    left, back = [], []
    for q in range(parts):
        rows = slice(q * chunk, (q + 1) * chunk)
        left += [np.concatenate([cos[rows], -sin[rows]], 1), np.concatenate([-sin[rows], -cos[rows]], 1)]
        back += [np.concatenate([cos[:, rows], sin[:, rows]], 0), np.concatenate([-sin[:, rows], cos[:, rows]], 0)]
    times = np.full((kept, 1), 2.0)
    times[0] = times[-1] = 1.0
    last = np.zeros((2 * HALF, length))
    last[:kept] = times * cos[:kept]
    last[HALF : HALF + kept] = -times * sin[:kept]
    return (
        first.astype(np.float32),
        np.concatenate(left, 0).astype(np.float32),
        np.concatenate(back, 1).astype(np.float32),
        last.astype(np.float32),
    )


def silu(values):
    half = 0.5 * values
    return half + half * jnp.tanh(half)


def tiled_eye(channels, lanes):
    lane = lax.broadcasted_iota(jnp.int32, (channels, lanes), 1)
    row = lax.broadcasted_iota(jnp.int32, (channels, lanes), 0)
    return ((lane & (channels - 1)) == row).astype(F32)


def across_rows(left, right):
    return lax.dot_general(left, right, (((0,), (0,)), ((), ())), preferred_element_type=F32)


def encode_kernel(
    across, down, kernel1, kernel2, bias1_in, bias2_in, first,
    feat, rowwise, hid, hidt, band1, band1t, band2, band2t, bias1, bias1t, bias2, bias2t,
):
    length = feat.shape[0]
    wide = across.shape[-1]
    lanes = band1.shape[1]
    cols = band2.shape[2]
    depth = band2.shape[1]
    channels = lanes // SPAN
    shift = channels.bit_length() - 1
    row_index, col_index = lax.axis_index("gy"), lax.axis_index("gx")
    ylo = jnp.where(row_index == 0, 1, 0)
    yhi = jnp.where(row_index == lax.axis_size("gy") - 1, length, length + 1)
    xlo = jnp.where(col_index == 0, 1, 0)
    xhi = jnp.where(col_index == lax.axis_size("gx") - 1, length, length + 1)

    eye = tiled_eye(channels, lanes)
    eye_bf = eye.astype(BF)
    for source, row_ref, col_ref, width in ((bias1_in, bias1, bias1t, lanes), (bias2_in, bias2, bias2t, cols)):
        spread = jnp.broadcast_to(source[...].astype(F32), (8, channels)).astype(BF)
        row = jnp.dot(spread, eye_bf[:, :width], preferred_element_type=F32)
        row_ref[...] = row
        col_ref[...] = jnp.transpose(jnp.broadcast_to(row[0:1], (128, width)))
    tap1 = across_rows(kernel1[...], eye_bf)
    unit = lax.shift_right_logical(lax.broadcasted_iota(jnp.int32, (2 * SPAN, lanes), 1), shift)
    gap = lax.broadcasted_iota(jnp.int32, (2 * SPAN, lanes), 0) - unit
    for ref, outer, inner in ((band1, 3, 1), (band1t, 1, 3)):
        parts = []
        for p in range(3):
            part = jnp.zeros((2 * SPAN, lanes), F32)
            for q in range(3):
                tap = outer * p + inner * q
                part = jnp.where(gap == q, tap1[tap : tap + 1], part)
            parts.append(part)
        whole = jnp.concatenate(parts, axis=0)
        if outer == 1:
            whole = jnp.transpose(whole)
        ref[...] = whole.astype(BF)
    tap2 = across_rows(kernel2[...], eye_bf[:, :cols])
    unit = lax.shift_right_logical(lax.broadcasted_iota(jnp.int32, (channels, cols), 1), shift)
    for a in range(3):
        for x in range(depth // channels):
            part = jnp.zeros((channels, cols), F32)
            for b in range(3):
                row = (3 * a + b) * channels
                part = jnp.where(unit == x - b, tap2[row : row + channels], part)
            band2[a, x * channels : (x + 1) * channels, :] = part.astype(BF)
    unit = lax.shift_right_logical(lax.broadcasted_iota(jnp.int32, (channels, depth), 1), shift)
    for b in range(3):
        taps = []
        for a in range(3):
            at = (3 * a + b) * channels
            taps.append(jnp.dot(kernel2[:, at : at + channels], eye_bf[:, :depth], preferred_element_type=F32))
        for y in range(cols // channels):
            part = jnp.zeros((channels, depth), F32)
            for a in range(3):
                part = jnp.where(unit == y + a, taps[a], part)
            band2t[b, y * channels : (y + 1) * channels, :] = part.astype(BF)

    def first_layer(blk, carry):
        r0 = pl.multiple_of(blk * SPAN, SPAN)
        c0 = pl.multiple_of(blk * lanes, lanes)
        rhs = jnp.concatenate([down[a, pl.ds(r0, 2 * SPAN), :] for a in range(3)], axis=0)
        summed = across_rows(rhs, band1[...])
        row = lax.broadcasted_iota(jnp.int32, (wide, 1), 0)
        col = r0 + lax.shift_right_logical(lax.broadcasted_iota(jnp.int32, (1, lanes), 1), shift)
        keep = ((row >= ylo) & (row <= yhi)).astype(F32) * ((col >= xlo) & (col <= xhi)).astype(F32)
        value = silu(summed + bias1[0:1]) * keep
        for a in range(3):
            hid[a, :, pl.ds(c0, lanes)] = value[a : a + length].astype(BF)

        rhs = jnp.concatenate([across[b, pl.ds(r0, 2 * SPAN), :] for b in range(3)], axis=0)
        summed = jnp.dot(band1t[...], rhs, preferred_element_type=F32)
        row = r0 + lax.shift_right_logical(lax.broadcasted_iota(jnp.int32, (lanes, 1), 0), shift)
        col = lax.broadcasted_iota(jnp.int32, (1, wide), 1)
        keep = ((row >= ylo) & (row <= yhi)).astype(F32) * ((col >= xlo) & (col <= xhi)).astype(F32)
        value = silu(summed + bias1t[:, 0:1]) * keep
        for b in range(3):
            hidt[b, pl.ds(c0, lanes), :] = value[:, b : b + length].astype(BF)
        return carry

    lax.fori_loop(0, wide // SPAN, first_layer, 0, unroll=wide // SPAN)

    def second_layer(blk, carry):
        c0 = pl.multiple_of(blk * cols, cols)
        window = jnp.concatenate([hid[a, :, pl.ds(c0, depth)] for a in range(3)], axis=1)
        acc = bias2[0:1] + jnp.dot(window, band2[...].reshape(3 * depth, cols), preferred_element_type=F32)
        feat[:, pl.ds(c0, cols)] = acc.astype(BF)
        window = jnp.concatenate([hidt[b, pl.ds(c0, depth), :] for b in range(3)], axis=0)
        band = jnp.concatenate([band2t[b] for b in range(3)], axis=1)
        acc = bias2t[:, 0:1] + jnp.dot(band, window, preferred_element_type=F32)
        pair = jnp.dot(acc.astype(BF), first[...], preferred_element_type=F32)
        rowwise[0, pl.ds(c0, cols), :] = pair[:, :HALF]
        rowwise[1, pl.ds(c0, cols), :] = pair[:, HALF:]
        return carry

    lax.fori_loop(0, length * channels // cols, second_layer, 0, unroll=4)


def mesh_kernel(
    channels, tissue, coarse, rowwise, tables, flow, nodes_out,
    left, spec, got, acc, owed, power, node, beside,
    send1, recv1, send2, recv2, send3, recv3,
):
    me = lax.axis_index("sec")
    secs = lax.axis_size("sec")
    row_index, rows_count = lax.axis_index("gy"), lax.axis_size("gy")
    col_index, cols_count = lax.axis_index("gx"), lax.axis_size("gx")
    length = rowwise.shape[1] // channels
    kept = length // 2 + 1
    double = 2 * length
    apart = -(-double // HALF) * HALF
    groups, size = spec.shape[1], spec.shape[2]
    half = size // 2
    peers = [lax.rem(me + r, secs) for r in range(1, secs)]
    targets = [{"sec": peer} for peer in peers]
    targets += [{"gy": lax.rem(row_index + 1, rows_count)}, {"gy": lax.rem(row_index + rows_count - 1, rows_count)}]
    targets += [{"gx": lax.rem(col_index + 1, cols_count)}, {"gx": lax.rem(col_index + cols_count - 1, cols_count)}]
    barrier = pltpu.get_barrier_semaphore()
    for target in targets:
        pl.semaphore_signal(barrier, inc=1, device_id=target, device_id_type=pl.DeviceIdType.MESH)
    left[...] = tables[:, :double].astype(BF)
    pl.semaphore_wait(barrier, len(targets))

    def spread(r, g):
        return pltpu.make_async_remote_copy(
            src_ref=spec.at[peers[r], g],
            dst_ref=got.at[me, g],
            send_sem=send1.at[r, g],
            recv_sem=recv1.at[r, g],
            device_id=targets[r],
            device_id_type=pl.DeviceIdType.MESH,
        )

    wide_lane = lax.broadcasted_iota(jnp.int32, (1, 2 * HALF), 1)
    own_mask = tissue[0].astype(F32)
    own = [coarse[0].astype(F32), coarse[1].astype(F32)]
    facts = jnp.zeros((1, 2 * HALF), F32)
    for place, fact in enumerate([own_mask] + own):
        facts = jnp.where(wide_lane == 3 * kept + place, fact, facts)

    def columns(g, carry):
        halves = []
        for q in range(2):
            packed = None
            for i in range(3):
                c = g * 3 + i
                value = rowwise[q, pl.ds(jnp.minimum(c, channels - 1), length, stride=channels), :]
                value = jnp.concatenate([value, jnp.zeros_like(value)], axis=1)
                if i == 0:
                    packed = value
                else:
                    value = value * (c < channels).astype(F32)
                    packed = packed + pltpu.roll(value, i * kept, 1)
            halves.append(packed.astype(BF))
        out = jnp.dot(left[...], jnp.concatenate(halves, axis=0), preferred_element_type=F32)
        out = (out + facts).astype(BF)
        for q in range(secs):
            spec[q, g] = out[q * size : (q + 1) * size]
        for r in range(secs - 1):
            spread(r, g).start()
        got[me, g] = spec[me, g]
        return carry

    lax.fori_loop(0, groups, columns, 0)
    acc[...] = jnp.zeros_like(acc)

    def multiply(g, carry):
        for r in range(secs - 1):
            spread(r, g).wait()
        values = [got[t, g].astype(F32) for t in range(secs)]
        for s in range(secs):
            for lag in range(1, min(s, LAGS) + 1):
                cur, ear = values[s], values[s - lag]
                acc[s, lag - 1, :half] += ear[:half] * cur[:half] + ear[half:] * cur[half:]
                acc[s, lag - 1, half:] += ear[:half] * cur[half:] - ear[half:] * cur[:half]
        return carry

    lax.fori_loop(0, groups, multiply, 0)
    for s in range(secs):
        for lag in range(LAGS):
            whole = acc[s, lag]
            total = whole[:, :HALF]
            for i in range(1, 3):
                total = total + pltpu.roll(whole, 2 * HALF - i * kept, 1)[:, :HALF]
            owed[s, lag] = total
    returns = [
        pltpu.make_async_remote_copy(
            src_ref=owed.at[peers[r]],
            dst_ref=power.at[me],
            send_sem=send2.at[r],
            recv_sem=recv2.at[r],
            device_id=targets[r],
            device_id_type=pl.DeviceIdType.MESH,
        )
        for r in range(secs - 1)
    ]
    for copy in returns:
        copy.start()
    power[me] = owed[me]

    row = lax.broadcasted_iota(jnp.int32, (length, 1), 0)
    col = lax.broadcasted_iota(jnp.int32, (1, length), 1)
    sign_y = jnp.where(row < length // 2, row, row - length).astype(F32)
    sign_x = jnp.where(col < length // 2, col, col - length).astype(F32)
    place = lax.broadcasted_iota(jnp.int32, flow.shape, 0)
    side = lax.broadcasted_iota(jnp.int32, flow.shape, 1)
    lane = lax.broadcasted_iota(jnp.int32, (1, HALF), 1)

    def pick(values, at):
        return jnp.sum(jnp.where(lane == at, values, 0.0))

    scale = 1.0 / (float(length) ** 3 * channels)
    for copy in returns:
        copy.wait()
    last = tables[: 2 * HALF, 2 * apart : 2 * apart + length]
    stacked = jnp.concatenate(
        [jnp.concatenate([power[q, lag] for q in range(secs)], axis=0) for lag in range(LAGS)], axis=1
    )
    mixed = jnp.dot(tables[:, apart : apart + double], stacked, precision=lax.Precision.HIGHEST, preferred_element_type=F32)
    result = jnp.zeros(flow.shape, F32)
    pulled = [jnp.float32(0.0), jnp.float32(0.0)]
    weights, goals = [], []
    at = 3 * kept - HALF
    for lag in range(LAGS):
        part = mixed[:, lag * HALF : (lag + 1) * HALF]
        lhs = jnp.concatenate([part[:length], part[length:]], axis=1)
        scores = jnp.dot(lhs, last, precision=lax.Precision.HIGHEST, preferred_element_type=F32) * scale
        chances = jnp.exp(scores - jnp.max(scores))
        total = jnp.sum(chances)
        usable = (me > lag).astype(F32)
        peak = [
            usable * (jnp.sum(chances * sign_y) / total),
            usable * (jnp.sum(chances * sign_x) / total),
        ]
        prior = got[lax.rem(me + secs - lag - 1, secs), 0, 0:16, HALF : 2 * HALF].astype(F32)[0:1]
        weight = usable * LAG_WEIGHTS[lag] * own_mask * pick(prior, at)
        goal = []
        for d in range(2):
            result = jnp.where((place == lag) & (side == d), peak[d], result)
            before = pick(prior, at + 1 + d)
            goal.append(peak[d] + own[d] - before)
            pulled[d] = pulled[d] + weight * (before + goal[d] - own[d])
        weights.append(weight)
        goals.append(goal)
    flow[...] = result
    current = jnp.zeros(node.shape, F32)
    for d in range(2):
        current = jnp.where(side == d, own[d] + STEP_SIZE * pulled[d], current)
    node[...] = current
    passes = [
        pltpu.make_async_remote_copy(
            src_ref=node,
            dst_ref=beside.at[k],
            send_sem=send3.at[k],
            recv_sem=recv3.at[k],
            device_id=target,
            device_id_type=pl.DeviceIdType.MESH,
        )
        for k, target in enumerate(targets)
    ]
    for copy in passes:
        copy.start()
    for copy in passes:
        copy.wait()
    pull = jnp.zeros(node.shape, F32)
    for lag in range(LAGS):
        goal = jnp.where(side == 0, goals[lag][0], goals[lag][1])
        pull = pull + weights[lag] * (beside[lag] + goal - current)
    inside = [row_index > 0, row_index < rows_count - 1, col_index > 0, col_index < cols_count - 1]
    plane = jnp.zeros(node.shape, F32)
    for k, here in enumerate(inside):
        plane = plane + here.astype(F32) * (beside[secs - 1 + k] - current)
    nodes_out[...] = current + STEP_SIZE * (pull + PLANE_STIFF * plane)


def body(sections, first_kernel, first_bias, second_kernel, second_bias, coarse, tissue):
    length = sections.shape[-1]
    channels = first_kernel.shape[0]
    secs = lax.axis_size("sec")
    first, left, back, last = make_tables(length, secs)
    wide = length + SPAN
    vmem = pl.BlockSpec(memory_space=pltpu.VMEM)
    dma = pltpu.SemaphoreType.DMA
    tall = wide + SPAN
    frame = jax.ShapeDtypeStruct((3, tall, wide), BF)
    across, down = pl.pallas_call(
        halo_kernel,
        out_shape=(frame, frame),
        in_specs=[vmem],
        out_specs=(vmem, vmem),
        scratch_shapes=[
            pltpu.VMEM((4, SPAN, length), BF),
            pltpu.VMEM((8, SPAN, length), BF),
            pltpu.VMEM((256, 256), F32),
            dma((8,)),
            dma((8,)),
        ],
        compiler_params=pltpu.CompilerParams(
            vmem_limit_bytes=8 * 1024 * 1024, collective_id=1, has_side_effects=True
        ),
        name="halo",
    )(sections[0])
    smem = pl.BlockSpec(memory_space=pltpu.SMEM)
    lanes, cols = SPAN * channels, SPAN // 2 * channels
    depth = 12 * channels
    features, rowwise = pl.pallas_call(
        encode_kernel,
        out_shape=(
            jax.ShapeDtypeStruct((length, length * channels), BF),
            jax.ShapeDtypeStruct((2, length * channels, HALF), F32),
        ),
        in_specs=[vmem] * 7,
        out_specs=(vmem, vmem),
        scratch_shapes=[
            pltpu.VMEM((3, length, wide * channels), BF),
            pltpu.VMEM((3, wide * channels, length), BF),
            pltpu.VMEM((6 * SPAN, lanes), BF),
            pltpu.VMEM((lanes, 6 * SPAN), BF),
            pltpu.VMEM((3, depth, cols), BF),
            pltpu.VMEM((3, cols, depth), BF),
            pltpu.VMEM((8, lanes), F32),
            pltpu.VMEM((lanes, 128), F32),
            pltpu.VMEM((8, cols), F32),
            pltpu.VMEM((cols, 128), F32),
        ],
        compiler_params=pltpu.CompilerParams(vmem_limit_bytes=26 * 1024 * 1024),
        name="encode",
    )(
        across, down, first_kernel, second_kernel, first_bias[None, :], second_bias[None, :],
        jnp.asarray(first, BF),
    )
    size = 2 * length // secs
    apart = -(-2 * length // HALF) * HALF
    joined = np.zeros((2 * length, 2 * apart + 2 * HALF), np.float32)
    joined[:, : 2 * length] = left
    joined[:, apart : apart + 2 * length] = back
    joined[: 2 * HALF, 2 * apart : 2 * apart + length] = last
    groups = (channels + 2) // 3
    others = secs - 1
    peaks, nodes = pl.pallas_call(
        functools.partial(mesh_kernel, channels),
        out_shape=(jax.ShapeDtypeStruct((8, 128), F32), jax.ShapeDtypeStruct((8, 128), F32)),
        in_specs=[smem, smem] + [vmem] * 2,
        out_specs=(vmem, vmem),
        scratch_shapes=[
            pltpu.VMEM(left.shape, BF),
            pltpu.VMEM((secs, groups, size, 2 * HALF), BF),
            pltpu.VMEM((secs, groups, size, 2 * HALF), BF),
            pltpu.VMEM((secs, LAGS, size, 2 * HALF), F32),
            pltpu.VMEM((secs, LAGS, size, HALF), F32),
            pltpu.VMEM((secs, LAGS, size, HALF), F32),
            pltpu.VMEM((8, 128), F32),
            pltpu.VMEM((others + 4, 8, 128), F32),
            dma((others, groups)),
            dma((others, groups)),
            dma((others,)),
            dma((others,)),
            dma((others + 4,)),
            dma((others + 4,)),
        ],
        compiler_params=pltpu.CompilerParams(
            vmem_limit_bytes=18 * 1024 * 1024, collective_id=0, has_side_effects=True
        ),
        name="mesh",
    )(
        tissue.reshape(1), coarse.reshape(2), rowwise, jnp.asarray(joined),
    )
    return (
        features.reshape(1, length, features.shape[-1]),
        peaks[:LAGS, :2].reshape(1, LAGS, 2, 1, 1),
        nodes[0, :2].reshape(1, 2, 1, 1),
    )


def solution(mesh):
    in_specs = (P("sec", "gy", "gx"), P(), P(), P(), P(), P("sec", None), P("sec", "gy", "gx"))
    out_specs = (P("sec", "gy", "gx"), P("sec", None, None, "gy", "gx"), P("sec", None, "gy", "gx"))
    return jax.shard_map(body, mesh=mesh, in_specs=in_specs, out_specs=out_specs, check_vma=False)
```

```python
import functools

import jax
import jax.numpy as jnp
import numpy as np
from jax import lax
from jax.experimental import pallas as pl
from jax.experimental.pallas import tpu as pltpu
from jax.sharding import PartitionSpec as P

LAGS = 3

LAG_WEIGHTS = (1.0, 0.5, 0.25)
STEP_SIZE = 0.3
PLANE_STIFF = 0.5
SPAN = 16
HALF = 128
BF = jnp.bfloat16
F32 = jnp.float32


def halo_kernel(image, across, down, strips, landed, ext, send, recv):
    length = image.shape[0]
    tall, wide = across.shape[1], across.shape[2]
    row_index, rows_count = lax.axis_index("gy"), lax.axis_size("gy")
    col_index, cols_count = lax.axis_index("gx"), lax.axis_size("gx")
    routes = [(dy, dx, 0 if dy < 0 else 1) for dy in (-1, 1) for dx in (-1, 0, 1)] + [(0, -1, 2), (0, 1, 3)]
    targets = [
        {
            "gy": lax.rem(row_index + dy + rows_count, rows_count),
            "gx": lax.rem(col_index + dx + cols_count, cols_count),
        }
        for dy, dx, _ in routes
    ]
    barrier = pltpu.get_barrier_semaphore()
    for target in targets:
        pl.semaphore_signal(barrier, inc=1, device_id=target, device_id_type=pl.DeviceIdType.MESH)
    own = image[...].astype(F32)
    turned = jnp.transpose(own)
    strips[0] = image[:SPAN]
    strips[1] = image[length - SPAN :]
    strips[2] = turned[:SPAN].astype(BF)
    strips[3] = turned[length - SPAN :].astype(BF)
    pl.semaphore_wait(barrier, len(targets))
    copies = [
        pltpu.make_async_remote_copy(
            src_ref=strips.at[strip],
            dst_ref=landed.at[k],
            send_sem=send.at[k],
            recv_sem=recv.at[k],
            device_id=targets[k],
            device_id_type=pl.DeviceIdType.MESH,
        )
        for k, (_, _, strip) in enumerate(routes)
    ]
    for copy in copies:
        copy.start()
    ext[...] = jnp.zeros_like(ext)
    ext[2 : length + 2, 2 : length + 2] = own
    for copy in copies:
        copy.wait()
    end = length + 2
    for k, (dy, dx, _) in enumerate(routes):
        here = jnp.logical_and(
            jnp.logical_and(row_index - dy >= 0, row_index - dy < rows_count),
            jnp.logical_and(col_index - dx >= 0, col_index - dx < cols_count),
        ).astype(F32)
        strip = landed[k].astype(F32) * here
        if dy == 0:
            strip = jnp.transpose(strip)
            if dx > 0:
                ext[2:end, 0:2] = strip[:, SPAN - 2 :]
            else:
                ext[2:end, end : end + 2] = strip[:, :2]
            continue
        part = strip[SPAN - 2 :] if dy > 0 else strip[:2]
        r0 = 0 if dy > 0 else end
        if dx == 0:
            ext[r0 : r0 + 2, 2:end] = part
        elif dx > 0:
            ext[r0 : r0 + 2, 0:2] = part[:, length - 2 :]
        else:
            ext[r0 : r0 + 2, end : end + 2] = part[:, :2]
    whole = ext[...]
    turned = jnp.transpose(whole)
    for k in range(3):
        across[k] = whole[:tall, k : k + wide].astype(BF)
        down[k] = turned[:tall, k : k + wide].astype(BF)


def make_tables(length, parts):
    ramp = np.arange(length)
    angle = (ramp[:, None] * ramp[None, :] % length) * (2.0 * np.pi / length)
    cos, sin = np.cos(angle), np.sin(angle)
    kept = length // 2 + 1
    first = np.zeros((length, 2 * HALF))
    first[:, :kept] = cos[:, :kept]
    first[:, HALF : HALF + kept] = sin[:, :kept]
    chunk = length // parts
    left, back = [], []
    for q in range(parts):
        rows = slice(q * chunk, (q + 1) * chunk)
        left += [np.concatenate([cos[rows], -sin[rows]], 1), np.concatenate([-sin[rows], -cos[rows]], 1)]
        back += [np.concatenate([cos[:, rows], sin[:, rows]], 0), np.concatenate([-sin[:, rows], cos[:, rows]], 0)]
    times = np.full((kept, 1), 2.0)
    times[0] = times[-1] = 1.0
    last = np.zeros((2 * HALF, length))
    last[:kept] = times * cos[:kept]
    last[HALF : HALF + kept] = -times * sin[:kept]
    return (
        first.astype(np.float32),
        np.concatenate(left, 0).astype(np.float32),
        np.concatenate(back, 1).astype(np.float32),
        last.astype(np.float32),
    )


def silu(values):
    half = 0.5 * values
    return half + half * jnp.tanh(half)


def tiled_eye(channels, lanes):
    lane = lax.broadcasted_iota(jnp.int32, (channels, lanes), 1)
    row = lax.broadcasted_iota(jnp.int32, (channels, lanes), 0)
    return ((lane & (channels - 1)) == row).astype(F32)


def across_rows(left, right):
    return lax.dot_general(left, right, (((0,), (0,)), ((), ())), preferred_element_type=F32)


def encode_kernel(
    across, down, kernel1, kernel2, bias1_in, bias2_in, first,
    feat, rowwise, hid, hidt, band1, band1t, band2, band2t, bias1, bias1t, bias2, bias2t,
):
    length = feat.shape[0]
    wide = across.shape[-1]
    lanes = band1.shape[1]
    cols = band2.shape[2]
    depth = band2.shape[1]
    channels = lanes // SPAN
    shift = channels.bit_length() - 1
    row_index, col_index = lax.axis_index("gy"), lax.axis_index("gx")
    ylo = jnp.where(row_index == 0, 1, 0)
    yhi = jnp.where(row_index == lax.axis_size("gy") - 1, length, length + 1)
    xlo = jnp.where(col_index == 0, 1, 0)
    xhi = jnp.where(col_index == lax.axis_size("gx") - 1, length, length + 1)

    eye = tiled_eye(channels, lanes)
    eye_bf = eye.astype(BF)
    for source, row_ref, col_ref, width in ((bias1_in, bias1, bias1t, lanes), (bias2_in, bias2, bias2t, cols)):
        spread = jnp.broadcast_to(source[...].astype(F32), (8, channels)).astype(BF)
        row = jnp.dot(spread, eye_bf[:, :width], preferred_element_type=F32)
        row_ref[...] = row
        col_ref[...] = jnp.transpose(jnp.broadcast_to(row[0:1], (128, width)))
    tap1 = across_rows(kernel1[...], eye_bf)
    unit = lax.shift_right_logical(lax.broadcasted_iota(jnp.int32, (2 * SPAN, lanes), 1), shift)
    gap = lax.broadcasted_iota(jnp.int32, (2 * SPAN, lanes), 0) - unit
    for ref, outer, inner in ((band1, 3, 1), (band1t, 1, 3)):
        parts = []
        for p in range(3):
            part = jnp.zeros((2 * SPAN, lanes), F32)
            for q in range(3):
                tap = outer * p + inner * q
                part = jnp.where(gap == q, tap1[tap : tap + 1], part)
            parts.append(part)
        whole = jnp.concatenate(parts, axis=0)
        if outer == 1:
            whole = jnp.transpose(whole)
        ref[...] = whole.astype(BF)
    tap2 = across_rows(kernel2[...], eye_bf[:, :cols])
    unit = lax.shift_right_logical(lax.broadcasted_iota(jnp.int32, (channels, cols), 1), shift)
    for a in range(3):
        for x in range(depth // channels):
            part = jnp.zeros((channels, cols), F32)
            for b in range(3):
                row = (3 * a + b) * channels
                part = jnp.where(unit == x - b, tap2[row : row + channels], part)
            band2[a, x * channels : (x + 1) * channels, :] = part.astype(BF)
    unit = lax.shift_right_logical(lax.broadcasted_iota(jnp.int32, (channels, depth), 1), shift)
    for b in range(3):
        taps = []
        for a in range(3):
            at = (3 * a + b) * channels
            taps.append(jnp.dot(kernel2[:, at : at + channels], eye_bf[:, :depth], preferred_element_type=F32))
        for y in range(cols // channels):
            part = jnp.zeros((channels, depth), F32)
            for a in range(3):
                part = jnp.where(unit == y + a, taps[a], part)
            band2t[b, y * channels : (y + 1) * channels, :] = part.astype(BF)

    def first_layer(blk, carry):
        r0 = pl.multiple_of(blk * SPAN, SPAN)
        c0 = pl.multiple_of(blk * lanes, lanes)
        rhs = jnp.concatenate([down[a, pl.ds(r0, 2 * SPAN), :] for a in range(3)], axis=0)
        summed = across_rows(rhs, band1[...])
        row = lax.broadcasted_iota(jnp.int32, (wide, 1), 0)
        col = r0 + lax.shift_right_logical(lax.broadcasted_iota(jnp.int32, (1, lanes), 1), shift)
        keep = ((row >= ylo) & (row <= yhi)).astype(F32) * ((col >= xlo) & (col <= xhi)).astype(F32)
        value = silu(summed + bias1[0:1]) * keep
        for a in range(3):
            hid[a, :, pl.ds(c0, lanes)] = value[a : a + length].astype(BF)

        rhs = jnp.concatenate([across[b, pl.ds(r0, 2 * SPAN), :] for b in range(3)], axis=0)
        summed = jnp.dot(band1t[...], rhs, preferred_element_type=F32)
        row = r0 + lax.shift_right_logical(lax.broadcasted_iota(jnp.int32, (lanes, 1), 0), shift)
        col = lax.broadcasted_iota(jnp.int32, (1, wide), 1)
        keep = ((row >= ylo) & (row <= yhi)).astype(F32) * ((col >= xlo) & (col <= xhi)).astype(F32)
        value = silu(summed + bias1t[:, 0:1]) * keep
        for b in range(3):
            hidt[b, pl.ds(c0, lanes), :] = value[:, b : b + length].astype(BF)
        return carry

    lax.fori_loop(0, wide // SPAN, first_layer, 0, unroll=wide // SPAN)

    def second_layer(blk, carry):
        c0 = pl.multiple_of(blk * cols, cols)
        window = jnp.concatenate([hid[a, :, pl.ds(c0, depth)] for a in range(3)], axis=1)
        acc = bias2[0:1] + jnp.dot(window, band2[...].reshape(3 * depth, cols), preferred_element_type=F32)
        feat[:, pl.ds(c0, cols)] = acc.astype(BF)
        window = jnp.concatenate([hidt[b, pl.ds(c0, depth), :] for b in range(3)], axis=0)
        band = jnp.concatenate([band2t[b] for b in range(3)], axis=1)
        acc = bias2t[:, 0:1] + jnp.dot(band, window, preferred_element_type=F32)
        pair = jnp.dot(acc.astype(BF), first[...], preferred_element_type=F32)
        rowwise[0, pl.ds(c0, cols), :] = pair[:, :HALF]
        rowwise[1, pl.ds(c0, cols), :] = pair[:, HALF:]
        return carry

    lax.fori_loop(0, length * channels // cols, second_layer, 0, unroll=10)


def mesh_kernel(
    channels, tissue, coarse, rowwise, tables, flow, nodes_out,
    left, spec, got, acc, owed, power, node, beside,
    send1, recv1, send2, recv2, send3, recv3,
):
    me = lax.axis_index("sec")
    secs = lax.axis_size("sec")
    row_index, rows_count = lax.axis_index("gy"), lax.axis_size("gy")
    col_index, cols_count = lax.axis_index("gx"), lax.axis_size("gx")
    length = rowwise.shape[1] // channels
    kept = length // 2 + 1
    double = 2 * length
    apart = -(-double // HALF) * HALF
    groups, size = spec.shape[1], spec.shape[2]
    half = size // 2
    peers = [lax.rem(me + r, secs) for r in range(1, secs)]
    targets = [{"sec": peer} for peer in peers]
    targets += [{"gy": lax.rem(row_index + 1, rows_count)}, {"gy": lax.rem(row_index + rows_count - 1, rows_count)}]
    targets += [{"gx": lax.rem(col_index + 1, cols_count)}, {"gx": lax.rem(col_index + cols_count - 1, cols_count)}]
    barrier = pltpu.get_barrier_semaphore()
    for target in targets:
        pl.semaphore_signal(barrier, inc=1, device_id=target, device_id_type=pl.DeviceIdType.MESH)
    left[...] = tables[:, :double].astype(BF)
    pl.semaphore_wait(barrier, len(targets))

    def spread(r, g):
        return pltpu.make_async_remote_copy(
            src_ref=spec.at[peers[r], g],
            dst_ref=got.at[me, g],
            send_sem=send1.at[r, g],
            recv_sem=recv1.at[r, g],
            device_id=targets[r],
            device_id_type=pl.DeviceIdType.MESH,
        )

    wide_lane = lax.broadcasted_iota(jnp.int32, (1, 2 * HALF), 1)
    own_mask = tissue[0].astype(F32)
    own = [coarse[0].astype(F32), coarse[1].astype(F32)]
    facts = jnp.zeros((1, 2 * HALF), F32)
    for place, fact in enumerate([own_mask] + own):
        facts = jnp.where(wide_lane == 3 * kept + place, fact, facts)

    def columns(g, carry):
        halves = []
        for q in range(2):
            packed = None
            for i in range(3):
                c = g * 3 + i
                value = rowwise[q, pl.ds(jnp.minimum(c, channels - 1), length, stride=channels), :]
                value = jnp.concatenate([value, jnp.zeros_like(value)], axis=1)
                if i == 0:
                    packed = value
                else:
                    value = value * (c < channels).astype(F32)
                    packed = packed + pltpu.roll(value, i * kept, 1)
            halves.append(packed.astype(BF))
        out = jnp.dot(left[...], jnp.concatenate(halves, axis=0), preferred_element_type=F32)
        out = (out + facts).astype(BF)
        for q in range(secs):
            spec[q, g] = out[q * size : (q + 1) * size]
        for r in range(secs - 1):
            spread(r, g).start()
        got[me, g] = spec[me, g]
        return carry

    lax.fori_loop(0, groups, columns, 0)
    acc[...] = jnp.zeros_like(acc)

    def multiply(g, carry):
        for r in range(secs - 1):
            spread(r, g).wait()
        values = [got[t, g].astype(F32) for t in range(secs)]
        for s in range(secs):
            for lag in range(1, min(s, LAGS) + 1):
                cur, ear = values[s], values[s - lag]
                acc[s, lag - 1, :half] += ear[:half] * cur[:half] + ear[half:] * cur[half:]
                acc[s, lag - 1, half:] += ear[:half] * cur[half:] - ear[half:] * cur[:half]
        return carry

    lax.fori_loop(0, groups, multiply, 0)
    for s in range(secs):
        for lag in range(LAGS):
            whole = acc[s, lag]
            total = whole[:, :HALF]
            for i in range(1, 3):
                total = total + pltpu.roll(whole, 2 * HALF - i * kept, 1)[:, :HALF]
            owed[s, lag] = total
    returns = [
        pltpu.make_async_remote_copy(
            src_ref=owed.at[peers[r]],
            dst_ref=power.at[me],
            send_sem=send2.at[r],
            recv_sem=recv2.at[r],
            device_id=targets[r],
            device_id_type=pl.DeviceIdType.MESH,
        )
        for r in range(secs - 1)
    ]
    for copy in returns:
        copy.start()
    power[me] = owed[me]

    row = lax.broadcasted_iota(jnp.int32, (length, 1), 0)
    col = lax.broadcasted_iota(jnp.int32, (1, length), 1)
    sign_y = jnp.where(row < length // 2, row, row - length).astype(F32)
    sign_x = jnp.where(col < length // 2, col, col - length).astype(F32)
    place = lax.broadcasted_iota(jnp.int32, flow.shape, 0)
    side = lax.broadcasted_iota(jnp.int32, flow.shape, 1)
    lane = lax.broadcasted_iota(jnp.int32, (1, HALF), 1)

    def pick(values, at):
        return jnp.sum(jnp.where(lane == at, values, 0.0))

    scale = 1.0 / (float(length) ** 3 * channels)
    for copy in returns:
        copy.wait()
    last = tables[: 2 * HALF, 2 * apart : 2 * apart + length]
    stacked = jnp.concatenate(
        [jnp.concatenate([power[q, lag] for q in range(secs)], axis=0) for lag in range(LAGS)], axis=1
    )
    mixed = jnp.dot(tables[:, apart : apart + double], stacked, precision=lax.Precision.HIGHEST, preferred_element_type=F32)
    result = jnp.zeros(flow.shape, F32)
    pulled = [jnp.float32(0.0), jnp.float32(0.0)]
    weights, goals = [], []
    at = 3 * kept - HALF
    for lag in range(LAGS):
        part = mixed[:, lag * HALF : (lag + 1) * HALF]
        lhs = jnp.concatenate([part[:length], part[length:]], axis=1)
        scores = jnp.dot(lhs, last, precision=lax.Precision.HIGHEST, preferred_element_type=F32) * scale
        chances = jnp.exp(scores - jnp.max(scores))
        total = jnp.sum(chances)
        usable = (me > lag).astype(F32)
        peak = [
            usable * (jnp.sum(chances * sign_y) / total),
            usable * (jnp.sum(chances * sign_x) / total),
        ]
        prior = got[lax.rem(me + secs - lag - 1, secs), 0, 0:16, HALF : 2 * HALF].astype(F32)[0:1]
        weight = usable * LAG_WEIGHTS[lag] * own_mask * pick(prior, at)
        goal = []
        for d in range(2):
            result = jnp.where((place == lag) & (side == d), peak[d], result)
            before = pick(prior, at + 1 + d)
            goal.append(peak[d] + own[d] - before)
            pulled[d] = pulled[d] + weight * (before + goal[d] - own[d])
        weights.append(weight)
        goals.append(goal)
    flow[...] = result
    current = jnp.zeros(node.shape, F32)
    for d in range(2):
        current = jnp.where(side == d, own[d] + STEP_SIZE * pulled[d], current)
    node[...] = current
    passes = [
        pltpu.make_async_remote_copy(
            src_ref=node,
            dst_ref=beside.at[k],
            send_sem=send3.at[k],
            recv_sem=recv3.at[k],
            device_id=target,
            device_id_type=pl.DeviceIdType.MESH,
        )
        for k, target in enumerate(targets)
    ]
    for copy in passes:
        copy.start()
    for copy in passes:
        copy.wait()
    pull = jnp.zeros(node.shape, F32)
    for lag in range(LAGS):
        goal = jnp.where(side == 0, goals[lag][0], goals[lag][1])
        pull = pull + weights[lag] * (beside[lag] + goal - current)
    inside = [row_index > 0, row_index < rows_count - 1, col_index > 0, col_index < cols_count - 1]
    plane = jnp.zeros(node.shape, F32)
    for k, here in enumerate(inside):
        plane = plane + here.astype(F32) * (beside[secs - 1 + k] - current)
    nodes_out[...] = current + STEP_SIZE * (pull + PLANE_STIFF * plane)


def body(sections, first_kernel, first_bias, second_kernel, second_bias, coarse, tissue):
    length = sections.shape[-1]
    channels = first_kernel.shape[0]
    secs = lax.axis_size("sec")
    first, left, back, last = make_tables(length, secs)
    wide = length + SPAN
    vmem = pl.BlockSpec(memory_space=pltpu.VMEM)
    dma = pltpu.SemaphoreType.DMA
    tall = wide + SPAN
    frame = jax.ShapeDtypeStruct((3, tall, wide), BF)
    across, down = pl.pallas_call(
        halo_kernel,
        out_shape=(frame, frame),
        in_specs=[vmem],
        out_specs=(vmem, vmem),
        scratch_shapes=[
            pltpu.VMEM((4, SPAN, length), BF),
            pltpu.VMEM((8, SPAN, length), BF),
            pltpu.VMEM((256, 256), F32),
            dma((8,)),
            dma((8,)),
        ],
        compiler_params=pltpu.CompilerParams(
            vmem_limit_bytes=8 * 1024 * 1024, collective_id=1, has_side_effects=True
        ),
        name="halo",
    )(sections[0])
    smem = pl.BlockSpec(memory_space=pltpu.SMEM)
    lanes, cols = SPAN * channels, SPAN // 2 * channels
    depth = 12 * channels
    features, rowwise = pl.pallas_call(
        encode_kernel,
        out_shape=(
            jax.ShapeDtypeStruct((length, length * channels), BF),
            jax.ShapeDtypeStruct((2, length * channels, HALF), F32),
        ),
        in_specs=[vmem] * 7,
        out_specs=(vmem, vmem),
        scratch_shapes=[
            pltpu.VMEM((3, length, wide * channels), BF),
            pltpu.VMEM((3, wide * channels, length), BF),
            pltpu.VMEM((6 * SPAN, lanes), BF),
            pltpu.VMEM((lanes, 6 * SPAN), BF),
            pltpu.VMEM((3, depth, cols), BF),
            pltpu.VMEM((3, cols, depth), BF),
            pltpu.VMEM((8, lanes), F32),
            pltpu.VMEM((lanes, 128), F32),
            pltpu.VMEM((8, cols), F32),
            pltpu.VMEM((cols, 128), F32),
        ],
        compiler_params=pltpu.CompilerParams(vmem_limit_bytes=26 * 1024 * 1024),
        name="encode",
    )(
        across, down, first_kernel, second_kernel, first_bias[None, :], second_bias[None, :],
        jnp.asarray(first, BF),
    )
    size = 2 * length // secs
    apart = -(-2 * length // HALF) * HALF
    joined = np.zeros((2 * length, 2 * apart + 2 * HALF), np.float32)
    joined[:, : 2 * length] = left
    joined[:, apart : apart + 2 * length] = back
    joined[: 2 * HALF, 2 * apart : 2 * apart + length] = last
    groups = (channels + 2) // 3
    others = secs - 1
    peaks, nodes = pl.pallas_call(
        functools.partial(mesh_kernel, channels),
        out_shape=(jax.ShapeDtypeStruct((8, 128), F32), jax.ShapeDtypeStruct((8, 128), F32)),
        in_specs=[smem, smem] + [vmem] * 2,
        out_specs=(vmem, vmem),
        scratch_shapes=[
            pltpu.VMEM(left.shape, BF),
            pltpu.VMEM((secs, groups, size, 2 * HALF), BF),
            pltpu.VMEM((secs, groups, size, 2 * HALF), BF),
            pltpu.VMEM((secs, LAGS, size, 2 * HALF), F32),
            pltpu.VMEM((secs, LAGS, size, HALF), F32),
            pltpu.VMEM((secs, LAGS, size, HALF), F32),
            pltpu.VMEM((8, 128), F32),
            pltpu.VMEM((others + 4, 8, 128), F32),
            dma((others, groups)),
            dma((others, groups)),
            dma((others,)),
            dma((others,)),
            dma((others + 4,)),
            dma((others + 4,)),
        ],
        compiler_params=pltpu.CompilerParams(
            vmem_limit_bytes=18 * 1024 * 1024, collective_id=0, has_side_effects=True
        ),
        name="mesh",
    )(
        tissue.reshape(1), coarse.reshape(2), rowwise, jnp.asarray(joined),
    )
    return (
        features.reshape(1, length, features.shape[-1]),
        peaks[:LAGS, :2].reshape(1, LAGS, 2, 1, 1),
        nodes[0, :2].reshape(1, 2, 1, 1),
    )


def solution(mesh):
    in_specs = (P("sec", "gy", "gx"), P(), P(), P(), P(), P("sec", None), P("sec", "gy", "gx"))
    out_specs = (P("sec", "gy", "gx"), P("sec", None, None, "gy", "gx"), P("sec", None, "gy", "gx"))
    return jax.shard_map(body, mesh=mesh, in_specs=in_specs, out_specs=out_specs, check_vma=False)
```
